512 devices in a mesh: dp: 64 (over y, z), tensor: 8 (over x, core).
Axes of the slice: x: 4, y: 4, z: 16, core: 2. Of those that a mesh axis runs over, the one named last changes fastest.
Arguments:
- grads: bfloat16 [64, 4096, 1024], P('dp', None, 'tensor'), may hold values from -70 to 70
- error: bfloat16 [64, 4096, 1024], P('dp', None, 'tensor'), may hold values from -3 to 3
- q_init: float32 [1024, 32], P('tensor'), may hold values from -6 to 6
Outputs:
- new_error: bfloat16 [64, 4096, 1024], P('dp', None, 'tensor')
- q_factor: float32 [1024, 32], P('tensor')
The draws below stay inside these ranges and needn't reach their ends.
All inputs are finite; a program needn't handle non-finite values.
Results may differ from the reference program's by a relative error of at most 0.0059.
Values may be sent and summed in bfloat16 or wider, within the bound.
A program may use at most 64 MiB of HBM per device.

```python
import jax
import jax.numpy as jnp
from jax import lax

R = 4096
COLS = 1024
RANK = 32
ITERS = 2
REPLICAS = 64


def draw_grads(key, part):
    key = jax.random.fold_in(key, 11)
    key_rows, key_cols, key_noise = jax.random.split(key, 3)
    row_scale = 10.0 ** (jax.random.uniform(key_rows, (R,), jnp.float32) - 0.5)
    col_scale = 10.0 ** (jax.random.uniform(key_cols, (COLS,), jnp.float32) - 0.5)
    noise = jnp.clip(jax.random.normal(key_noise, (REPLICAS, R, COLS), jnp.float32), -5.0, 5.0)
    return (noise * row_scale[None, :, None] * col_scale[None, None, :]).astype(jnp.bfloat16)


def block_scale(key, extent, cuts, smallest, top_value):
    gain = 1.0
    for dim, blocks in cuts:
        heights = jax.random.uniform(jax.random.fold_in(jax.random.fold_in(key, 6), dim), (blocks,), jnp.float32, smallest / len(cuts), top_value / len(cuts))
        gain = gain * jnp.repeat(jnp.exp(heights), extent[dim] // blocks).reshape((-1,) + (1,) * (len(extent) - 1 - dim))
    return gain


def gaussian(own_key, extent, spread, most, cuts=(), kind=jnp.bfloat16):
    array = jax.random.normal(own_key, extent, jnp.float32) * spread
    if len(cuts) > 0:
        array = block_scale(own_key, extent, cuts, -0.22, 0.18) * array
    return jnp.clip(array, min=-most, max=most).astype(kind)


def setup_inputs(seed: int = 0) -> dict:
    arg_keys = jax.random.split(jax.random.key(seed), 4)
    return {
        "grads": draw_grads(jax.random.fold_in(arg_keys[3], 71), 0),
        "error": gaussian(arg_keys[1], (REPLICAS, R, COLS), 0.5, 3.0, ((0, 64), (2, 8))),
        "q_init": gaussian(arg_keys[2], (COLS, RANK), 1.0, 6.0, ((0, 8),), jnp.float32),
    }


def orthonormal(p_sum):
    gram_matrix = jnp.dot(p_sum.T, p_sum, precision=lax.Precision.HIGHEST)
    lower_factor = jnp.linalg.cholesky(gram_matrix)
    p_hat = lax.linalg.triangular_solve(lower_factor, p_sum, left_side=False, lower=True, transpose_a=True)
    return p_hat.astype(jnp.bfloat16)

def reference(grads, error, q_init):
    accumulated = (grads.astype(jnp.float32) + error.astype(jnp.float32)).astype(jnp.bfloat16)
    q_factor = q_init
    p_basis = jnp.zeros((R, RANK), jnp.bfloat16)
    for iteration in range(ITERS):
        q_round = q_factor.astype(jnp.bfloat16)

        def add_left(total, matrix):
            return (total + jnp.dot(matrix.astype(jnp.float32), q_round.astype(jnp.float32), preferred_element_type=jnp.float32), None)
        p_sum = lax.scan(add_left, jnp.zeros((R, RANK), jnp.float32), accumulated)[0]
        p_basis = orthonormal(p_sum)

        def add_right(total, matrix):
            return (total + jnp.dot(matrix.T.astype(jnp.float32), p_basis.astype(jnp.float32), preferred_element_type=jnp.float32), None)
        q_factor = lax.scan(add_right, jnp.zeros((COLS, RANK), jnp.float32), accumulated)[0] / REPLICAS
    approx = jnp.dot(p_basis.astype(jnp.float32), q_factor.T, precision=lax.Precision.HIGHEST)
    new_error = (accumulated.astype(jnp.float32) - approx[None]).astype(jnp.bfloat16)
    return (new_error, q_factor)
```

```python
import functools

import jax
import jax.numpy as jnp
from jax import lax
from jax.experimental import pallas as pl
from jax.experimental.pallas import tpu as pltpu
from jax.sharding import PartitionSpec as P

MESH = pl.DeviceIdType.MESH
HIGHEST = lax.Precision.HIGHEST
ITERS = 2
RANK = 32
ROWS = 64
COLS = 128
TILES = 5
F32, BF16 = jnp.float32, jnp.bfloat16


def kernel(
    ny, nz, nt,
    grads, error, q_init, new_error, q_out,
    g_buf, e_buf, acc, y_buf, z_send, z_buf, a_sum, t_buf, send_tiles, r_buf, x_buf, out_tiles, p_own, p_all, m_buf,
    load_sem, y_send_sem, y_sem, z_send_sem, z_sem, t_send_sem, t_sem, r_send_sem, r_sem, x_send_sem, x_sem,
    o_send_sem, o_sem, pz_send_sem, pz_sem, py_send_sem, py_sem, store_sem,
):
    dp, t = lax.axis_index("dp"), lax.axis_index("tensor")
    y, z = lax.div(dp, nz), lax.rem(dp, nz)

    def remote(src, dst, send, recv, y_, z_, t_):
        return pltpu.make_async_remote_copy(
            src_ref=src, dst_ref=dst, send_sem=send, recv_sem=recv,
            device_id=(y_ * nz + z_, t_), device_id_type=MESH,
        )

    def got(ref, sem):
        remote(ref, ref, sem, sem, y, z, t).wait_recv()

    def sent(ref, sem):
        remote(ref, ref, sem, sem, y, z, t).wait_send()

    def y_peer(j):
        return lax.rem(y + j, ny)

    def z_peer(j):
        return lax.rem(z + j, nz)

    def t_peer(j):
        return lax.rem(t + j, nt)

    def target(i):
        half = lax.div(i + 1, 2)
        return lax.rem(z + nz // 2 + (1 - 2 * lax.rem(i, 2)) * half + nz, nz)

    def loads(i):
        zt = target(i)
        rows = pl.ds(pl.multiple_of(zt * (ny * ROWS), ny * ROWS), ny * ROWS)
        return (
            pltpu.make_async_copy(grads.at[0, rows, :], g_buf.at[i], load_sem.at[0, i]),
            pltpu.make_async_copy(error.at[0, rows, :], e_buf.at[i], load_sem.at[1, i]),
        )

    @pl.loop(0, nz)
    def _(i):
        for load in loads(i):
            load.start()

    barrier = pltpu.get_barrier_semaphore()
    for j in range(1, ny):
        pl.semaphore_signal(barrier, inc=1, device_id=(y_peer(j) * nz + z, t), device_id_type=MESH)
    for j in range(1, nz):
        pl.semaphore_signal(barrier, inc=1, device_id=(y * nz + z_peer(j), t), device_id_type=MESH)
    for j in range(1, nt):
        pl.semaphore_signal(barrier, inc=1, device_id=(dp, t_peer(j)), device_id_type=MESH)
    pl.semaphore_wait(barrier, (ny - 1) + (nz - 1) + (nt - 1))

    @pl.loop(0, nz)
    def _(i):
        for load in loads(i):
            load.wait()
        zt = target(i)
        total = (g_buf[i].astype(F32) + e_buf[i].astype(F32)).astype(BF16)
        acc[zt] = total.reshape(ny, ROWS, COLS)
        for j in range(1, ny):
            remote(acc.at[zt, y_peer(j)], y_buf.at[i, j - 1], y_send_sem, y_sem.at[i], y_peer(j), z, t).start()

    def y_total(i):
        got(y_buf.at[i], y_sem.at[i])
        total = acc[target(i), y].astype(F32)
        for j in range(ny - 1):
            total = total + y_buf[i, j].astype(F32)
        return total

    @pl.loop(0, nz - 1)
    def _(i):
        z_send[i] = y_total(i).astype(BF16)
        remote(z_send.at[i], z_buf.at[i], z_send_sem, z_sem, y, target(i), t).start()

    a_own = y_total(nz - 1)
    q_rows = q_init[...].T.astype(BF16)
    got(z_buf, z_sem)
    for i in range(nz - 1):
        a_own = a_own + z_buf[i].astype(F32)
    a_sum[...] = a_own

    lane16 = lax.broadcasted_iota(jnp.int32, (RANK // 2, 128), 1)
    lane32 = lax.broadcasted_iota(jnp.int32, (RANK, 128), 1)
    row32 = lax.broadcasted_iota(jnp.int32, (RANK, 128), 0)

    for it in range(ITERS):
        a = a_sum[...]
        a_high = a.astype(BF16)
        a_low = (a - a_high.astype(F32)).astype(BF16)
        parts = lax.dot_general(
            q_rows, jnp.concatenate([a_high, a_low], axis=0), (((1,), (1,)), ((), ())), preferred_element_type=F32
        )
        both = parts + pltpu.roll(parts, ROWS, 1)
        t_buf[it, t] = jnp.where(lane16 < ROWS, both[: RANK // 2], both[RANK // 2 :])
        for j in range(1, nt):
            remote(t_buf.at[it, t], t_buf.at[it, t], t_send_sem.at[it], t_sem.at[it], y, z, t_peer(j)).start()
        got(t_buf.at[it, pl.ds(0, nt - 1)], t_sem.at[it])
        p_packed = t_buf[it, 0]
        for j in range(1, nt):
            p_packed = p_packed + t_buf[it, j]
        p_rows = jnp.concatenate([p_packed, pltpu.roll(p_packed, ROWS, 1)], axis=0)[:, :ROWS]

        q_part = jnp.dot(p_rows, a, precision=HIGHEST, preferred_element_type=F32)
        gram_part = lax.dot_general(
            p_rows, p_rows, (((1,), (1,)), ((), ())), precision=HIGHEST, preferred_element_type=F32
        )
        for k in range(4):
            send_tiles[it, k] = q_part[8 * k : 8 * (k + 1)]
        send_tiles[it, 4] = jnp.concatenate([gram_part[8 * k : 8 * (k + 1)] for k in range(4)], axis=1)
        for k in range(TILES):
            zk = (k * nz) // TILES
            here = z == zk

            @pl.when(here)
            def _():
                r_buf[it, z] = send_tiles[it, k]

            @pl.when(jnp.logical_not(here))
            def _():
                remote(
                    send_tiles.at[it, k], r_buf.at[it, z], r_send_sem.at[it], r_sem.at[it], y, zk, t
                ).start()

        if it == ITERS - 1:
            p_own[...] = p_packed.astype(BF16)
            p_all[z, y] = p_own[...]

            @pl.loop(1, nz)
            def _(j):
                remote(p_own, p_all.at[z, y], pz_send_sem, pz_sem, y, z_peer(j), t).start()

        for k in range(TILES):
            zk = (k * nz) // TILES

            @pl.when(z == zk)
            def _():
                got(r_buf.at[it, pl.ds(0, nz - 1)], r_sem.at[it])
                total = r_buf[it, 0]
                for j in range(1, nz):
                    total = total + r_buf[it, j]
                x_buf[it, y] = total
                for j in range(1, ny):
                    remote(
                        x_buf.at[it, y], x_buf.at[it, y], x_send_sem.at[it], x_sem.at[it], y_peer(j), z, t
                    ).start()
                got(x_buf.at[it, pl.ds(0, ny - 1)], x_sem.at[it])
                total = x_buf[it, 0]
                for j in range(1, ny):
                    total = total + x_buf[it, j]
                out_tiles[it, k] = total
                for j in range(1, nz):
                    remote(
                        out_tiles.at[it, k], out_tiles.at[it, k], o_send_sem.at[it], o_sem.at[it, k], y, z_peer(j), t
                    ).start()

        if it == ITERS - 1:
            got(p_all.at[pl.ds(0, nz - 1), 0], pz_sem)
            for j in range(1, ny):
                remote(p_all.at[:, y], p_all.at[:, y], py_send_sem, py_sem, y_peer(j), z, t).start()

        for k in range(TILES):
            zk = (k * nz) // TILES

            @pl.when(z != zk)
            def _():
                got(out_tiles.at[it, k], o_sem.at[it, k])

        packed = out_tiles[it, 4]
        work = jnp.concatenate(
            [packed] + [pltpu.roll(packed, 128 - RANK * k, 1) for k in range(1, 4)], axis=0
        )
        lower = jnp.concatenate([out_tiles[it, k] for k in range(4)], axis=0)
        full = lower
        for k in range(RANK):
            column = jnp.broadcast_to(work[:, k : k + 1], (RANK, 128))
            inverse = 1.0 / column[k : k + 1]
            factor = jnp.where(row32 == k, 0.0, column * inverse)
            below = jnp.where(row32 > k, factor, 0.0)
            last = it == ITERS - 1
            if last:
                full = full - factor * full[k : k + 1]
            lower = lower - below * lower[k : k + 1]
            if k < RANK - 1:
                work = work - (factor if last else below) * work[k : k + 1]
        diagonal = jnp.sum(jnp.where(lane32 == row32, work, 0.0), axis=1, keepdims=True)
        q_next = lower / (jnp.sqrt(diagonal) * (ny * nz))
        q_rows = q_next.astype(BF16)
        if it == ITERS - 1:
            m = full / (diagonal * (ny * nz))
            q_out[...] = q_next.T

    m_high = m.astype(BF16)
    m_low = (m - m_high.astype(F32)).astype(BF16)
    half = RANK // 2
    m_buf[...] = jnp.concatenate(
        [
            jnp.concatenate([m_high[:half], m_high[half:]], axis=1),
            jnp.concatenate([m_low[:half], m_low[half:]], axis=1),
        ],
        axis=0,
    )
    got(p_all.at[:, pl.ds(0, ny - 1)], py_sem)

    @pl.loop(0, nz)
    def _(i):
        for yy in range(ny):
            tile = p_all[i, yy]
            doubled = jnp.concatenate([tile, tile], axis=0)
            product = lax.dot_general(
                doubled, m_buf[...], (((0,), (0,)), ((), ())), preferred_element_type=F32
            )
            approx = product[:ROWS, :COLS] + product[ROWS:, COLS:]
            g_buf[i, pl.ds(yy * ROWS, ROWS), :] = (acc[i, yy].astype(F32) - approx).astype(BF16)
        rows = pl.ds(pl.multiple_of(i * (ny * ROWS), ny * ROWS), ny * ROWS)
        pltpu.make_async_copy(g_buf.at[i], new_error.at[0, rows, :], store_sem).start()

    sent(acc.at[:, pl.ds(0, ny - 1)], y_send_sem)
    sent(z_send, z_send_sem)
    for it in range(ITERS):
        sent(t_buf.at[it, pl.ds(0, nt - 1)], t_send_sem.at[it])
        reducer = functools.reduce(jnp.logical_or, [z == (k * nz) // TILES for k in range(TILES)])

        @pl.when(reducer)
        def _():
            sent(send_tiles.at[it, pl.ds(0, TILES - 1)], r_send_sem.at[it])
            sent(x_buf.at[it, pl.ds(0, ny - 1)], x_send_sem.at[it])
            sent(r_buf.at[it, pl.ds(0, nz - 1)], o_send_sem.at[it])

        @pl.when(jnp.logical_not(reducer))
        def _():
            sent(send_tiles.at[it], r_send_sem.at[it])

    sent(p_all.at[pl.ds(0, nz - 1), 0], pz_send_sem)
    sent(p_all.at[:, pl.ds(0, ny - 1)], py_send_sem)
    pltpu.make_async_copy(g_buf, g_buf, store_sem).wait()


def on_device(ny, nz, nt, grads, error, q_init):
    rows = ny * nz * ROWS
    dma = pltpu.SemaphoreType.DMA
    return pl.pallas_call(
        functools.partial(kernel, ny, nz, nt),
        out_shape=(
            jax.ShapeDtypeStruct((1, rows, COLS), BF16),
            jax.ShapeDtypeStruct((COLS, RANK), F32),
        ),
        in_specs=[
            pl.BlockSpec(memory_space=pl.ANY),
            pl.BlockSpec(memory_space=pl.ANY),
            pl.BlockSpec(memory_space=pltpu.VMEM),
        ],
        out_specs=(pl.BlockSpec(memory_space=pl.ANY), pl.BlockSpec(memory_space=pltpu.VMEM)),
        scratch_shapes=[
            pltpu.VMEM((nz, ny * ROWS, COLS), BF16),
            pltpu.VMEM((nz, ny * ROWS, COLS), BF16),
            pltpu.VMEM((nz, ny, ROWS, COLS), BF16),
            pltpu.VMEM((nz, ny - 1, ROWS, COLS), BF16),
            pltpu.VMEM((nz - 1, ROWS, COLS), BF16),
            pltpu.VMEM((nz - 1, ROWS, COLS), BF16),
            pltpu.VMEM((ROWS, COLS), F32),
            pltpu.VMEM((ITERS, nt, RANK // 2, 128), F32),
            pltpu.VMEM((ITERS, TILES, 8, 128), F32),
            pltpu.VMEM((ITERS, nz, 8, 128), F32),
            pltpu.VMEM((ITERS, ny, 8, 128), F32),
            pltpu.VMEM((ITERS, TILES, 8, 128), F32),
            pltpu.VMEM((RANK // 2, 128), BF16),
            pltpu.VMEM((nz, ny, RANK // 2, 128), BF16),
            pltpu.VMEM((RANK, 2 * COLS), BF16),
            dma((2, nz)), dma, dma((nz,)), dma, dma, dma((ITERS,)), dma((ITERS,)), dma((ITERS,)), dma((ITERS,)),
            dma((ITERS,)), dma((ITERS,)), dma((ITERS,)), dma((ITERS, TILES)), dma, dma, dma, dma, dma,
        ],
        compiler_params=pltpu.CompilerParams(
            collective_id=0, has_side_effects=True, vmem_limit_bytes=32 * 1024 * 1024
        ),
    )(grads, error, q_init)


def solution(mesh, ny=4):
    nz, nt = mesh.shape["dp"] // ny, mesh.shape["tensor"]
    return jax.shard_map(
        functools.partial(on_device, ny, nz, nt),
        mesh=mesh,
        in_specs=(P("dp", None, "tensor"), P("dp", None, "tensor"), P("tensor", None)),
        out_specs=(P("dp", None, "tensor"), P("tensor", None)),
        check_vma=False,
    )
```

```python
import functools

import jax
import jax.numpy as jnp
from jax import lax
from jax.experimental import pallas as pl
from jax.experimental.pallas import tpu as pltpu
from jax.sharding import PartitionSpec as P

MESH = pl.DeviceIdType.MESH
HIGHEST = lax.Precision.HIGHEST
RANK = 32
BLOCK = 64
PARTS = 2
PART = BLOCK // PARTS
GROUP = 4
COLS = 128
SUMS = 40
F32, BF16 = jnp.float32, jnp.bfloat16


def eliminate(gram_packed, right, both_sides):
    row = lax.broadcasted_iota(jnp.int32, (RANK, 128), 0)
    lane = lax.broadcasted_iota(jnp.int32, (RANK, 128), 1)
    work = jnp.concatenate(
        [gram_packed] + [pltpu.roll(gram_packed, 128 - RANK * k, 1) for k in range(1, RANK // 8)], axis=0
    )
    lower, full = right, right
    for k in range(RANK):
        column = jnp.broadcast_to(work[:, k : k + 1], (RANK, 128))
        inverse = 1.0 / column[k : k + 1]
        factor = jnp.where(row == k, 0.0, column * inverse)
        below = jnp.where(row > k, factor, 0.0)
        if both_sides:
            full = full - factor * full[k : k + 1]
        lower = lower - below * lower[k : k + 1]
        if k < RANK - 1:
            work = work - (factor if both_sides else below) * work[k : k + 1]
    diagonal = jnp.sum(jnp.where(lane == row, work, 0.0), axis=1, keepdims=True)
    return diagonal, lower, full


def kernel(
    ny, nz, nt,
    grads, error, q_init, new_error, q_out,
    g_buf, e_buf, acc, y_buf, z_send, z_buf, a_all, t_buf, p1_all, s_buf, part_buf, c_buf, x_buf, p2_all, p_rows,
    load_sem, y_send_sem, y_sem, z_send_sem, z_sem, a_send_sem, a_sem, t_send_sem, t_sem, p_send_sem, p_sem,
    s_send_sem, s_sem, c_send_sem, c_sem, x_send_sem, x_sem, store_sem,
):
    nx = nt // 2
    dp, t = lax.axis_index("dp"), lax.axis_index("tensor")
    y, z = lax.div(dp, nz), lax.rem(dp, nz)
    x, core = lax.div(t, 2), lax.rem(t, 2)
    other = 1 - core
    sibling = x * 2 + other
    half = nz * BLOCK // 2

    def remote(src, dst, send, recv, y_, z_, t_):
        return pltpu.make_async_remote_copy(
            src_ref=src, dst_ref=dst, send_sem=send, recv_sem=recv,
            device_id=(y_ * nz + z_, t_), device_id_type=MESH,
        )

    def got(ref, sem):
        remote(ref, ref, sem, sem, y, z, t).wait_recv()

    def sent(ref, sem):
        remote(ref, ref, sem, sem, y, z, t).wait_send()

    def y_peer(j):
        return lax.rem(y + j, ny)

    def t_peer(j):
        return lax.rem(t + j, nt)

    def target(i):
        return lax.rem(z + nz // 2 + (1 - 2 * lax.rem(i, 2)) * lax.div(i + 1, 2) + nz, nz)

    def loads(i):
        zt = target(i)
        return (
            pltpu.make_async_copy(grads.at[:, zt], g_buf.at[i], load_sem.at[0, i]),
            pltpu.make_async_copy(error.at[:, zt], e_buf.at[i], load_sem.at[1, i]),
        )

    barrier = pltpu.get_barrier_semaphore()

    @pl.loop(0, nz - 1)
    def _(i):
        pl.semaphore_signal(barrier, inc=1, device_id=(y * nz + target(i), t), device_id_type=MESH)

    for j in range(1, ny):
        pl.semaphore_signal(barrier, inc=1, device_id=(y_peer(j) * nz + z, t), device_id_type=MESH)
    for j in range(1, nt):
        pl.semaphore_signal(barrier, inc=1, device_id=(dp, t_peer(j)), device_id_type=MESH)

    @pl.loop(0, nz)
    def _(i):
        for load in loads(i):
            load.start()

    at_the_end = []

    def rows_of(h):
        return pl.ds(h * PART, PART)

    def send_y(h, g):
        group = pl.ds(g * GROUP, GROUP)
        for j in range(1, ny):
            remote(
                acc.at[group, y_peer(j), rows_of(h)], y_buf.at[h, group, j - 1],
                y_send_sem, y_sem.at[h, g], y_peer(j), z, t,
            ).start()

    def accumulate(g):
        @pl.loop(g * GROUP, (g + 1) * GROUP)
        def _(i):
            for load in loads(i):
                load.wait()
            acc[i] = (g_buf[i].astype(F32) + e_buf[i].astype(F32)).astype(BF16)

    accumulate(0)
    pl.semaphore_wait(barrier, (ny - 1) + (nz - 1) + (nt - 1))
    send_y(0, 0)

    @pl.loop(1, nz // GROUP)
    def _(g):
        accumulate(g)
        send_y(0, g)

    for h in range(1, PARTS):

        @pl.loop(0, nz // GROUP)
        def _(g):
            send_y(h, g)

    at_the_end.append(lambda: sent(acc.at[:, pl.ds(0, ny - 1)], y_send_sem))

    def y_total(h, i):
        total = acc[i, y, h * PART : (h + 1) * PART].astype(F32)
        for j in range(ny - 1):
            total = total + y_buf[h, i, j].astype(F32)
        return total

    own = []
    for h in range(PARTS):

        @pl.loop(0, nz // GROUP)
        def _(g):
            got(y_buf.at[h, pl.ds(g * GROUP, GROUP)], y_sem.at[h, g])

            @pl.loop(g * GROUP, lax.min((g + 1) * GROUP, nz - 1))
            def _(i):
                z_send[h, i] = y_total(h, i).astype(BF16)
                remote(z_send.at[h, i], z_buf.at[h, i], z_send_sem, z_sem.at[h], y, target(i), t).start()

        own.append(y_total(h, nz - 1))
    at_the_end.append(lambda: sent(z_send, z_send_sem))

    for h in range(PARTS):
        got(z_buf.at[h], z_sem.at[h])
        total = own[h]
        for i in range(nz - 1):
            total = total + z_buf[h, i].astype(F32)
        a_all[z, h * PART : (h + 1) * PART] = total.astype(BF16)
        mine = a_all.at[z, rows_of(h)]

        @pl.loop(0, nz - 1)
        def _(i):
            remote(mine, mine, a_send_sem, a_sem, y, target(i), t).start()

    at_the_end.append(lambda: sent(a_all.at[pl.ds(0, nz - 1)], a_send_sem))

    lane16 = lax.broadcasted_iota(jnp.int32, (RANK // 2, 128), 1)
    q_rows = q_init[...].astype(BF16)
    block = a_all[z]
    p_part = lax.dot_general(
        q_rows, jnp.concatenate([block, block], axis=0), (((1,), (1,)), ((), ())), preferred_element_type=F32
    )
    t_buf[t] = jnp.where(lane16 < BLOCK, p_part[: RANK // 2], p_part[RANK // 2 :])
    for j in range(1, nt):
        remote(t_buf.at[t], t_buf.at[t], t_send_sem, t_sem, y, z, t_peer(j)).start()
    at_the_end.append(lambda: sent(t_buf.at[pl.ds(0, nt - 1)], t_send_sem))
    got(t_buf.at[pl.ds(0, nt - 1)], t_sem)
    p_packed = t_buf[0]
    for j in range(1, nt):
        p_packed = p_packed + t_buf[j]
    p1_all[z] = p_packed.astype(BF16)

    @pl.loop(0, nz - 1)
    def _(i):
        remote(p1_all.at[z], p1_all.at[z], p_send_sem, p_sem, y, target(i), t).start()

    at_the_end.append(lambda: sent(p1_all.at[pl.ds(0, nz - 1)], p_send_sem))
    got(a_all.at[pl.ds(0, nz - 1)], a_sem)
    got(p1_all.at[pl.ds(0, nz - 1)], p_sem)
    a = a_all[...].reshape(nz * BLOCK, COLS)
    columns = []
    for m in range(nz // 2):
        first, second = p1_all[2 * m].astype(F32), p1_all[2 * m + 1].astype(F32)
        top = jnp.where(lane16 < BLOCK, first, pltpu.roll(second, BLOCK, 1))
        bottom = jnp.where(lane16 < BLOCK, pltpu.roll(first, BLOCK, 1), second)
        columns.append(jnp.concatenate([top, bottom], axis=0))
    p1 = jnp.concatenate(columns, axis=1).astype(BF16)

    def sum_over_y(it, q_part, gram_part):
        s_buf[it, y, :RANK] = q_part
        s_buf[it, y, RANK:] = jnp.concatenate([gram_part[8 * k : 8 * (k + 1)] for k in range(RANK // 8)], axis=1)
        for j in range(1, ny):
            remote(s_buf.at[it, y], s_buf.at[it, y], s_send_sem.at[it], s_sem.at[it], y_peer(j), z, t).start()
        at_the_end.append(lambda: sent(s_buf.at[it, pl.ds(0, ny - 1)], s_send_sem.at[it]))

    def summed_over_y(it):
        got(s_buf.at[it, pl.ds(0, ny - 1)], s_sem.at[it])
        total = s_buf[it, 0]
        for j in range(1, ny):
            total = total + s_buf[it, j]
        return total[:RANK], total[RANK:]

    sum_over_y(
        0,
        jnp.dot(p1, a, preferred_element_type=F32),
        lax.dot_general(p1, p1, (((1,), (1,)), ((), ())), preferred_element_type=F32),
    )
    right, gram = summed_over_y(0)
    diagonal, lower, _ = eliminate(gram, right, False)
    q_rows = (lower / (jnp.sqrt(diagonal) * (ny * nz))).astype(BF16)

    p_part = lax.dot_general(q_rows, a, (((1,), (1,)), ((), ())), preferred_element_type=F32)
    part_buf[0] = p_part[:, :half]
    part_buf[1] = p_part[:, half:]
    remote(part_buf.at[other], c_buf, c_send_sem.at[0], c_sem.at[0], y, z, sibling).start()
    at_the_end.append(lambda: sent(c_buf, c_send_sem.at[0]))
    got(c_buf, c_sem.at[0])
    x_buf[x] = part_buf[core] + c_buf[...]
    for j in range(1, nx):
        remote(x_buf.at[x], x_buf.at[x], x_send_sem, x_sem, y, z, lax.rem(x + j, nx) * 2 + core).start()
    at_the_end.append(lambda: sent(x_buf.at[pl.ds(0, nx - 1)], x_send_sem))
    got(x_buf.at[pl.ds(0, nx - 1)], x_sem)
    p_half = x_buf[0]
    for j in range(1, nx):
        p_half = p_half + x_buf[j]
    p2_all[y, core] = p_half
    mine = p2_all.at[y, core]
    remote(mine, mine, c_send_sem.at[1], c_sem.at[1], y, z, sibling).start()
    at_the_end.append(lambda: sent(c_buf, c_send_sem.at[1]))
    for j in range(1, ny):
        remote(mine, mine, s_send_sem.at[2], s_sem.at[2], y_peer(j), z, t).start()
    at_the_end.append(lambda: sent(p2_all.at[pl.ds(0, ny - 1), 0], s_send_sem.at[2]))
    got(p2_all.at[y, other], c_sem.at[1])
    p2 = jnp.concatenate([p2_all[y, 0], p2_all[y, 1]], axis=1)
    p2_high = p2.astype(BF16)
    p2_low = (p2 - p2_high.astype(F32)).astype(BF16)
    both = jnp.dot(jnp.concatenate([p2_high, p2_low], axis=0), a, preferred_element_type=F32)
    sum_over_y(
        1,
        both[:RANK] + both[RANK:],
        lax.dot_general(p2, p2, (((1,), (1,)), ((), ())), precision=HIGHEST, preferred_element_type=F32),
    )

    got(p2_all.at[pl.ds(0, ny - 1), 0], s_sem.at[2])
    for j in range(1, ny):
        theirs = p2_all.at[y_peer(j), core]
        remote(theirs, theirs, c_send_sem.at[2], c_sem.at[2], y, z, sibling).start()
    at_the_end.append(lambda: sent(p2_all.at[pl.ds(0, ny - 1), 0], c_send_sem.at[2]))
    right, gram = summed_over_y(1)
    got(p2_all.at[pl.ds(0, ny - 1), 0], c_sem.at[2])

    for yy in range(ny):
        for c in range(2):

            @pl.loop(0, half // 128)
            def _(b):
                tile = p2_all[yy, c, :, pl.ds(pl.multiple_of(b * 128, 128), 128)]
                high = tile.astype(BF16)
                low = (tile - high.astype(F32)).astype(BF16)
                start = yy * 2 * half + c * half + b * 128
                p_rows[pl.ds(pl.multiple_of(start, 128), 128)] = jnp.concatenate([high, low, high, low], axis=0).T

    diagonal, lower, full = eliminate(gram, right, True)
    q_out[...] = lower / (jnp.sqrt(diagonal) * (ny * nz))
    m = full / (diagonal * (ny * nz))
    m_high = m.astype(BF16)
    m_low = (m - m_high.astype(F32)).astype(BF16)
    m_rows = jnp.concatenate([m_high, m_high, m_low, m_low], axis=0)

    @pl.loop(0, nz)
    def _(i):
        zt = target(i)
        left = jnp.concatenate(
            [p_rows[pl.ds(pl.multiple_of((yy * nz + zt) * BLOCK, BLOCK), BLOCK)] for yy in range(ny)], axis=0
        )
        approx = jnp.dot(left, m_rows, preferred_element_type=F32).reshape(ny, BLOCK, COLS)
        g_buf[i] = (acc[i].astype(F32) - approx).astype(BF16)
        pltpu.make_async_copy(g_buf.at[i], new_error.at[:, zt], store_sem).start()

    for wait in at_the_end:
        wait()
    pltpu.make_async_copy(g_buf, g_buf, store_sem).wait()


def on_device(ny, nz, nt, grads, error, q_init):
    dma = pltpu.SemaphoreType.DMA
    blocks = (ny, nz, BLOCK, COLS)
    half = nz * BLOCK // 2
    new_error, q_rows = pl.pallas_call(
        functools.partial(kernel, ny, nz, nt),
        out_shape=(jax.ShapeDtypeStruct(blocks, BF16), jax.ShapeDtypeStruct((RANK, COLS), F32)),
        in_specs=[
            pl.BlockSpec(memory_space=pl.ANY),
            pl.BlockSpec(memory_space=pl.ANY),
            pl.BlockSpec(memory_space=pltpu.VMEM),
        ],
        out_specs=(pl.BlockSpec(memory_space=pl.ANY), pl.BlockSpec(memory_space=pltpu.VMEM)),
        scratch_shapes=[
            pltpu.VMEM((nz, ny, BLOCK, COLS), BF16),
            pltpu.VMEM((nz, ny, BLOCK, COLS), BF16),
            pltpu.VMEM((nz, ny, BLOCK, COLS), BF16),
            pltpu.VMEM((PARTS, nz, ny - 1, PART, COLS), BF16),
            pltpu.VMEM((PARTS, nz - 1, PART, COLS), BF16),
            pltpu.VMEM((PARTS, nz - 1, PART, COLS), BF16),
            pltpu.VMEM((nz, BLOCK, COLS), BF16),
            pltpu.VMEM((nt, RANK // 2, 128), F32),
            pltpu.VMEM((nz, RANK // 2, 128), BF16),
            pltpu.VMEM((2, ny, SUMS, 128), F32),
            pltpu.VMEM((2, RANK, half), F32),
            pltpu.VMEM((RANK, half), F32),
            pltpu.VMEM((nt // 2, RANK, half), F32),
            pltpu.VMEM((ny, 2, RANK, half), F32),
            pltpu.VMEM((ny * nz * BLOCK, 4 * RANK), BF16),
            dma((2, nz)), dma, dma((PARTS, nz // GROUP)), dma, dma((PARTS,)), dma, dma, dma, dma, dma, dma,
            dma((3,)), dma((3,)), dma((3,)), dma((3,)), dma, dma, dma,
        ],
        compiler_params=pltpu.CompilerParams(
            collective_id=0, has_side_effects=True, vmem_limit_bytes=60 * 1024 * 1024
        ),
    )(grads.reshape(blocks), error.reshape(blocks), q_init.T)
    return new_error.reshape(1, ny * nz * BLOCK, COLS), q_rows.T


def solution(mesh, ny=4):
    nz, nt = mesh.shape["dp"] // ny, mesh.shape["tensor"]
    return jax.shard_map(
        functools.partial(on_device, ny, nz, nt),
        mesh=mesh,
        in_specs=(P("dp", None, "tensor"), P("dp", None, "tensor"), P("tensor", None)),
        out_specs=(P("dp", None, "tensor"), P("tensor", None)),
        check_vma=False,
    )
```

```python
import functools

import jax
import jax.numpy as jnp
from jax import lax
from jax.experimental import pallas as pl
from jax.experimental.pallas import tpu as pltpu
from jax.sharding import PartitionSpec as P

MESH = pl.DeviceIdType.MESH
HIGHEST = lax.Precision.HIGHEST
RANK = 32
BLOCK = 64
PARTS = 2
PART = BLOCK // PARTS
STEPS = 8
GROUP = 2
COLS = 128
SUMS = 40
F32, BF16 = jnp.float32, jnp.bfloat16


def eliminate(gram_packed, right, both_sides):
    row = lax.broadcasted_iota(jnp.int32, (8, 128), 0)
    lane = lax.broadcasted_iota(jnp.int32, (8, 128), 1)
    tiles = RANK // 8
    work = [gram_packed if r == 0 else pltpu.roll(gram_packed, 128 - RANK * r, 1) for r in range(tiles)]
    lower = [right[8 * r : 8 * (r + 1)] for r in range(tiles)]
    full = list(lower)
    diagonal = [jnp.zeros((8, 128), F32)] * tiles
    for first in range(0, RANK, STEPS):
        columns = [
            [jnp.broadcast_to(work[r][:, first + j : first + j + 1], (8, 128)) for r in range(tiles)]
            for j in range(STEPS)
        ]
        for j in range(STEPS):
            k = first + j
            own, at = k // 8, k % 8
            pivot = columns[j][own][at : at + 1]
            inverse = 1.0 / pivot
            diagonal[own] = jnp.where(row == at, pivot, diagonal[own])
            factor, below = [], []
            for r in range(tiles):
                scaled = columns[j][r] * inverse
                factor.append(jnp.where(row == at, 0.0, scaled) if r == own else scaled)
                below.append(jnp.where(row > at, scaled, 0.0) if r == own else scaled)

            def step(matrix, factors, start):
                pivot_row = matrix[own][at : at + 1]
                for r in range(start, tiles):
                    matrix[r] = matrix[r] - factors[r] * pivot_row

            both = (factor, 0) if both_sides else (below, own)
            for later in columns[j + 1 :]:
                step(later, *both)
            step(lower, below, own)
            if both_sides:
                step(full, factor, 0)
            step(work, *both)
    return tuple(jnp.concatenate(m, axis=0) for m in (diagonal, lower, full))


def kernel(
    ny, nz, nt,
    grads, error, q_init, new_error, q_out,
    g_buf, e_buf, acc, y_buf, z_send, z_buf, a_all, t_buf, p1_all, s_buf, part_buf, c_buf, x_buf, p2_all, p_rows,
    load_sem, y_send_sem, y_sem, z_send_sem, z_sem, a_send_sem, a_sem, t_send_sem, t_sem, p_send_sem, p_sem,
    s_send_sem, s_sem, c_send_sem, c_sem, x_send_sem, x_sem, store_sem, ready,
):
    nx = nt // 2
    dp, t = lax.axis_index("dp"), lax.axis_index("tensor")
    y, z = lax.div(dp, nz), lax.rem(dp, nz)
    x, core = lax.div(t, 2), lax.rem(t, 2)
    other = 1 - core
    sibling = x * 2 + other
    half = nz * BLOCK // 2

    def remote(src, dst, send, recv, y_, z_, t_):
        return pltpu.make_async_remote_copy(
            src_ref=src, dst_ref=dst, send_sem=send, recv_sem=recv,
            device_id=(y_ * nz + z_, t_), device_id_type=MESH,
        )

    def got(ref, sem):
        remote(ref, ref, sem, sem, y, z, t).wait_recv()

    def sent(ref, sem):
        remote(ref, ref, sem, sem, y, z, t).wait_send()

    def y_peer(j):
        return lax.rem(y + j, ny)

    def t_peer(j):
        return lax.rem(t + j, nt)

    def target(i):
        return lax.rem(z + nz // 2 + (1 - 2 * lax.rem(i, 2)) * lax.div(i + 1, 2) + nz, nz)

    def loads(i):
        zt = target(i)
        return (
            pltpu.make_async_copy(grads.at[:, zt], g_buf.at[i], load_sem.at[0, i]),
            pltpu.make_async_copy(error.at[:, zt], e_buf.at[i], load_sem.at[1, i]),
        )

    barrier = pltpu.get_barrier_semaphore()

    def enter(y_, z_, t_):
        pl.semaphore_signal(barrier, inc=1, device_id=(y_ * nz + z_, t_), device_id_type=MESH)

    @pl.loop(0, nz - 1)
    def _(i):
        enter(y, target(i), x * 2 + 1)

    for j in range(1, ny):
        enter(y_peer(j), z, x * 2)
    for j in range(1, nx):
        enter(y, z, lax.rem(x + j, nx) * 2 + 1)
    enter(y, z, sibling)

    @pl.loop(0, nz)
    def _(i):
        for load in loads(i):
            load.start()

    at_the_end = []

    def rows_of(h):
        return pl.ds(h * PART, PART)

    def send_y(h, g):
        group = pl.ds(g * GROUP, GROUP)
        for j in range(1, ny):
            remote(
                acc.at[group, y_peer(j), rows_of(h)], y_buf.at[h, group, j - 1],
                y_send_sem, y_sem.at[h, g], y_peer(j), z, t,
            ).start()

    def accumulate(g):
        @pl.loop(g * GROUP, (g + 1) * GROUP)
        def _(i):
            for load in loads(i):
                load.wait()
            acc[i] = (g_buf[i].astype(F32) + e_buf[i].astype(F32)).astype(BF16)

    accumulate(0)

    def entered(here, count):
        @pl.when(core == here)
        def _():
            pl.semaphore_wait(barrier, count)
            pl.semaphore_signal(ready, inc=1, device_id=(dp, sibling), device_id_type=MESH)

        @pl.when(core != here)
        def _():
            pl.semaphore_wait(ready, 1)

    entered(0, 2 * (ny - 1) + 1)
    send_y(0, 0)

    @pl.loop(1, nz // GROUP)
    def _(g):
        accumulate(g)
        send_y(0, g)

    for h in range(1, PARTS):

        @pl.loop(0, nz // GROUP)
        def _(g):
            send_y(h, g)

    at_the_end.append(lambda: sent(acc.at[:, pl.ds(0, ny - 1)], y_send_sem))

    def y_total(h, i):
        total = acc[i, y, h * PART : (h + 1) * PART].astype(F32)
        for j in range(ny - 1):
            total = total + y_buf[h, i, j].astype(F32)
        return total

    entered(1, 2 * (nz - 1) + 2 * (nx - 1) + 1)
    own = []
    for h in range(PARTS):

        @pl.loop(0, nz // GROUP)
        def _(g):
            got(y_buf.at[h, pl.ds(g * GROUP, GROUP)], y_sem.at[h, g])

            @pl.loop(g * GROUP, lax.min((g + 1) * GROUP, nz - 1))
            def _(i):
                z_send[h, i] = y_total(h, i).astype(BF16)
                remote(z_send.at[h, i], z_buf.at[h, i], z_send_sem, z_sem.at[h], y, target(i), t).start()

        own.append(y_total(h, nz - 1))
    at_the_end.append(lambda: sent(z_send, z_send_sem))

    for h in range(PARTS):
        got(z_buf.at[h], z_sem.at[h])
        total = own[h]
        for i in range(nz - 1):
            total = total + z_buf[h, i].astype(F32)
        a_all[z, h * PART : (h + 1) * PART] = total.astype(BF16)
        mine = a_all.at[z, rows_of(h)]

        @pl.loop(0, nz - 1)
        def _(i):
            remote(mine, mine, a_send_sem, a_sem, y, target(i), t).start()

    at_the_end.append(lambda: sent(a_all.at[pl.ds(0, nz - 1)], a_send_sem))

    lane16 = lax.broadcasted_iota(jnp.int32, (RANK // 2, 128), 1)
    q_rows = q_init[...].astype(BF16)
    block = a_all[z]
    p_part = lax.dot_general(
        q_rows, jnp.concatenate([block, block], axis=0), (((1,), (1,)), ((), ())), preferred_element_type=F32
    )
    t_buf[t] = jnp.where(lane16 < BLOCK, p_part[: RANK // 2], p_part[RANK // 2 :])
    for j in range(1, nt):
        remote(t_buf.at[t], t_buf.at[t], t_send_sem, t_sem, y, z, t_peer(j)).start()
    at_the_end.append(lambda: sent(t_buf.at[pl.ds(0, nt - 1)], t_send_sem))
    got(t_buf.at[pl.ds(0, nt - 1)], t_sem)
    p_packed = t_buf[0]
    for j in range(1, nt):
        p_packed = p_packed + t_buf[j]
    p1_all[z] = p_packed.astype(BF16)

    @pl.loop(0, nz - 1)
    def _(i):
        remote(p1_all.at[z], p1_all.at[z], p_send_sem, p_sem, y, target(i), t).start()

    at_the_end.append(lambda: sent(p1_all.at[pl.ds(0, nz - 1)], p_send_sem))
    got(a_all.at[pl.ds(0, nz - 1)], a_sem)
    got(p1_all.at[pl.ds(0, nz - 1)], p_sem)
    a = a_all[...].reshape(nz * BLOCK, COLS)
    columns = []
    for m in range(nz // 2):
        first, second = p1_all[2 * m].astype(F32), p1_all[2 * m + 1].astype(F32)
        top = jnp.where(lane16 < BLOCK, first, pltpu.roll(second, BLOCK, 1))
        bottom = jnp.where(lane16 < BLOCK, pltpu.roll(first, BLOCK, 1), second)
        columns.append(jnp.concatenate([top, bottom], axis=0))
    p1 = jnp.concatenate(columns, axis=1).astype(BF16)

    def sum_over_y(it, q_part, gram_part):
        s_buf[it, y, :RANK] = q_part
        s_buf[it, y, RANK:] = jnp.concatenate([gram_part[8 * k : 8 * (k + 1)] for k in range(RANK // 8)], axis=1)
        for j in range(1, ny):
            remote(s_buf.at[it, y], s_buf.at[it, y], s_send_sem.at[it], s_sem.at[it], y_peer(j), z, t).start()
        at_the_end.append(lambda: sent(s_buf.at[it, pl.ds(0, ny - 1)], s_send_sem.at[it]))

    def summed_over_y(it):
        got(s_buf.at[it, pl.ds(0, ny - 1)], s_sem.at[it])
        total = s_buf[it, 0]
        for j in range(1, ny):
            total = total + s_buf[it, j]
        return total[:RANK], total[RANK:]

    sum_over_y(
        0,
        jnp.dot(p1, a, preferred_element_type=F32),
        lax.dot_general(p1, p1, (((1,), (1,)), ((), ())), preferred_element_type=F32),
    )
    right, gram = summed_over_y(0)
    diagonal, lower, _ = eliminate(gram, right, False)
    q_rows = (lower / (jnp.sqrt(diagonal) * (ny * nz))).astype(BF16)

    p_part = lax.dot_general(q_rows, a, (((1,), (1,)), ((), ())), preferred_element_type=F32)
    part_buf[0] = p_part[:, :half]
    part_buf[1] = p_part[:, half:]
    remote(part_buf.at[other], c_buf, c_send_sem.at[0], c_sem.at[0], y, z, sibling).start()
    at_the_end.append(lambda: sent(c_buf, c_send_sem.at[0]))
    got(c_buf, c_sem.at[0])
    x_buf[x] = part_buf[core] + c_buf[...]
    for j in range(1, nx):
        remote(x_buf.at[x], x_buf.at[x], x_send_sem, x_sem, y, z, lax.rem(x + j, nx) * 2 + core).start()
    at_the_end.append(lambda: sent(x_buf.at[pl.ds(0, nx - 1)], x_send_sem))
    got(x_buf.at[pl.ds(0, nx - 1)], x_sem)
    p_half = x_buf[0]
    for j in range(1, nx):
        p_half = p_half + x_buf[j]
    p2_all[y, core] = p_half
    mine = p2_all.at[y, core]
    remote(mine, mine, c_send_sem.at[1], c_sem.at[1], y, z, sibling).start()
    at_the_end.append(lambda: sent(c_buf, c_send_sem.at[1]))
    for j in range(1, ny):
        remote(mine, mine, s_send_sem.at[2], s_sem.at[2], y_peer(j), z, t).start()
    at_the_end.append(lambda: sent(p2_all.at[pl.ds(0, ny - 1), 0], s_send_sem.at[2]))
    got(p2_all.at[y, other], c_sem.at[1])
    p2 = jnp.concatenate([p2_all[y, 0], p2_all[y, 1]], axis=1)
    p2_high = p2.astype(BF16)
    p2_low = (p2 - p2_high.astype(F32)).astype(BF16)
    both = jnp.dot(jnp.concatenate([p2_high, p2_low], axis=0), a, preferred_element_type=F32)
    sum_over_y(
        1,
        both[:RANK] + both[RANK:],
        lax.dot_general(p2, p2, (((1,), (1,)), ((), ())), precision=HIGHEST, preferred_element_type=F32),
    )

    def spread(yy, c):
        for b in range(half // 128):
            tile = p2_all[yy, c, :, b * 128 : (b + 1) * 128]
            high = tile.astype(BF16)
            low = (tile - high.astype(F32)).astype(BF16)
            start = yy * 2 * half + c * half + b * 128
            p_rows[pl.ds(pl.multiple_of(start, 128), 128)] = jnp.concatenate([high, low, high, low], axis=0).T

    for c in range(2):
        spread(y, c)

    got(p2_all.at[pl.ds(0, ny - 1), 0], s_sem.at[2])
    for j in range(1, ny):
        theirs = p2_all.at[y_peer(j), core]
        remote(theirs, theirs, c_send_sem.at[2], c_sem.at[2], y, z, sibling).start()
    at_the_end.append(lambda: sent(p2_all.at[pl.ds(0, ny - 1), 0], c_send_sem.at[2]))
    right, gram = summed_over_y(1)
    got(p2_all.at[pl.ds(0, ny - 1), 0], c_sem.at[2])
    for j in range(1, ny):
        for c in range(2):
            spread(y_peer(j), c)
    diagonal, lower, full = eliminate(gram, right, True)
    q_out[...] = lower / (jnp.sqrt(diagonal) * (ny * nz))
    m = full / (diagonal * (ny * nz))
    m_high = m.astype(BF16)
    m_low = (m - m_high.astype(F32)).astype(BF16)
    m_rows = jnp.concatenate([m_high, m_high, m_low, m_low], axis=0)

    @pl.loop(0, nz, unroll=4)
    def _(i):
        zt = target(i)
        left = jnp.concatenate(
            [p_rows[pl.ds(pl.multiple_of((yy * nz + zt) * BLOCK, BLOCK), BLOCK)] for yy in range(ny)], axis=0
        )
        approx = jnp.dot(left, m_rows, preferred_element_type=F32).reshape(ny, BLOCK, COLS)
        g_buf[i] = (acc[i].astype(F32) - approx).astype(BF16)
        pltpu.make_async_copy(g_buf.at[i], new_error.at[:, zt], store_sem).start()

    for wait in at_the_end:
        wait()
    pltpu.make_async_copy(g_buf, g_buf, store_sem).wait()


def on_device(ny, nz, nt, grads, error, q_init):
    dma = pltpu.SemaphoreType.DMA
    blocks = (ny, nz, BLOCK, COLS)
    half = nz * BLOCK // 2
    new_error, q_rows = pl.pallas_call(
        functools.partial(kernel, ny, nz, nt),
        out_shape=(jax.ShapeDtypeStruct(blocks, BF16), jax.ShapeDtypeStruct((RANK, COLS), F32)),
        in_specs=[
            pl.BlockSpec(memory_space=pl.ANY),
            pl.BlockSpec(memory_space=pl.ANY),
            pl.BlockSpec(memory_space=pltpu.VMEM),
        ],
        out_specs=(pl.BlockSpec(memory_space=pl.ANY), pl.BlockSpec(memory_space=pltpu.VMEM)),
        scratch_shapes=[
            pltpu.VMEM((nz, ny, BLOCK, COLS), BF16),
            pltpu.VMEM((nz, ny, BLOCK, COLS), BF16),
            pltpu.VMEM((nz, ny, BLOCK, COLS), BF16),
            pltpu.VMEM((PARTS, nz, ny - 1, PART, COLS), BF16),
            pltpu.VMEM((PARTS, nz - 1, PART, COLS), BF16),
            pltpu.VMEM((PARTS, nz - 1, PART, COLS), BF16),
            pltpu.VMEM((nz, BLOCK, COLS), BF16),
            pltpu.VMEM((nt, RANK // 2, 128), F32),
            pltpu.VMEM((nz, RANK // 2, 128), BF16),
            pltpu.VMEM((2, ny, SUMS, 128), F32),
            pltpu.VMEM((2, RANK, half), F32),
            pltpu.VMEM((RANK, half), F32),
            pltpu.VMEM((nt // 2, RANK, half), F32),
            pltpu.VMEM((ny, 2, RANK, half), F32),
            pltpu.VMEM((ny * nz * BLOCK, 4 * RANK), BF16),
            dma((2, nz)), dma, dma((PARTS, nz // GROUP)), dma, dma((PARTS,)), dma, dma, dma, dma, dma, dma,
            dma((3,)), dma((3,)), dma((3,)), dma((3,)), dma, dma, dma, pltpu.SemaphoreType.REGULAR,
        ],
        compiler_params=pltpu.CompilerParams(
            collective_id=0, has_side_effects=True, vmem_limit_bytes=52 * 1024 * 1024
        ),
    )(grads.reshape(blocks), error.reshape(blocks), q_init.T)
    return new_error.reshape(1, ny * nz * BLOCK, COLS), q_rows.T


def solution(mesh, ny=4):
    nz, nt = mesh.shape["dp"] // ny, mesh.shape["tensor"]
    return jax.shard_map(
        functools.partial(on_device, ny, nz, nt),
        mesh=mesh,
        in_specs=(P("dp", None, "tensor"), P("dp", None, "tensor"), P("tensor", None)),
        out_specs=(P("dp", None, "tensor"), P("tensor", None)),
        check_vma=False,
    )
```

```python
import functools

import jax
import jax.numpy as jnp
from jax import lax
from jax.experimental import pallas as pl
from jax.experimental.pallas import tpu as pltpu
from jax.sharding import PartitionSpec as P

MESH = pl.DeviceIdType.MESH
HIGHEST = lax.Precision.HIGHEST
RANK = 32
BLOCK = 64
CUTS = (0, 32, BLOCK)
PARTS = len(CUTS) - 1
STEPS = 8
GROUP = 2
COLS = 128
SUMS = 40
F32, BF16 = jnp.float32, jnp.bfloat16


def eliminate(gram_packed, right, both_sides):
    row = lax.broadcasted_iota(jnp.int32, (8, 128), 0)
    lane = lax.broadcasted_iota(jnp.int32, (8, 128), 1)
    tiles = RANK // 8
    work = [gram_packed if r == 0 else pltpu.roll(gram_packed, 128 - RANK * r, 1) for r in range(tiles)]
    lower = [right[8 * r : 8 * (r + 1)] for r in range(tiles)]
    full = list(lower)
    diagonal = [jnp.zeros((8, 128), F32)] * tiles
    for first in range(0, RANK, STEPS):
        columns = [
            [jnp.broadcast_to(work[r][:, first + j : first + j + 1], (8, 128)) for r in range(tiles)]
            for j in range(STEPS)
        ]
        for j in range(STEPS):
            k = first + j
            own, at = k // 8, k % 8
            pivot = columns[j][own][at : at + 1]
            inverse = 1.0 / pivot
            diagonal[own] = jnp.where(row == at, pivot, diagonal[own])
            factor, below = [], []
            for r in range(tiles):
                scaled = columns[j][r] * inverse
                factor.append(jnp.where(row == at, 0.0, scaled) if r == own else scaled)
                below.append(jnp.where(row > at, scaled, 0.0) if r == own else scaled)

            def step(matrix, factors, start):
                pivot_row = matrix[own][at : at + 1]
                for r in range(start, tiles):
                    matrix[r] = matrix[r] - factors[r] * pivot_row

            both = (factor, 0) if both_sides else (below, own)
            for later in columns[j + 1 :]:
                step(later, *both)
            step(lower, below, own)
            if both_sides:
                step(full, factor, 0)
            step(work, *both)
    return tuple(jnp.concatenate(m, axis=0) for m in (diagonal, lower, full))


def kernel(
    ny, nz, nt,
    grads, error, q_init, new_error, q_out,
    g_buf, e_buf, acc, y_buf, z_send, z_buf, a_all, t_buf, p1_all, s_buf, part_buf, c_buf, x_buf, p2_all, p_rows,
    load_sem, y_send_sem, y_sem, z_send_sem, z_sem, a_send_sem, a_sem, t_send_sem, t_sem, p_send_sem, p_sem,
    s_send_sem, s_sem, c_send_sem, c_sem, x_send_sem, x_sem, ready,
):
    nx = nt // 2
    dp, t = lax.axis_index("dp"), lax.axis_index("tensor")
    y, z = lax.div(dp, nz), lax.rem(dp, nz)
    x, core = lax.div(t, 2), lax.rem(t, 2)
    other = 1 - core
    sibling = x * 2 + other
    half = nz * BLOCK // 2

    def remote(src, dst, send, recv, y_, z_, t_):
        return pltpu.make_async_remote_copy(
            src_ref=src, dst_ref=dst, send_sem=send, recv_sem=recv,
            device_id=(y_ * nz + z_, t_), device_id_type=MESH,
        )

    def got(ref, sem):
        remote(ref, ref, sem, sem, y, z, t).wait_recv()

    def sent(ref, sem):
        remote(ref, ref, sem, sem, y, z, t).wait_send()

    def y_peer(j):
        return lax.rem(y + j, ny)

    def t_peer(j):
        return lax.rem(t + j, nt)

    def target(i):
        return lax.rem(z + nz // 2 + (1 - 2 * lax.rem(i, 2)) * lax.div(i + 1, 2) + nz, nz)

    def loads(i):
        zt = target(i)
        return (
            pltpu.make_async_copy(grads.at[:, zt], g_buf.at[i], load_sem.at[0, i]),
            pltpu.make_async_copy(error.at[:, zt], e_buf.at[i], load_sem.at[1, i]),
        )

    barrier = pltpu.get_barrier_semaphore()

    def enter(y_, z_, t_):
        pl.semaphore_signal(barrier, inc=1, device_id=(y_ * nz + z_, t_), device_id_type=MESH)

    for j in range(1, ny):
        enter(y_peer(j), z, x * 2)
    enter(y, z, sibling)

    @pl.loop(0, nz)
    def _(i):
        for load in loads(i):
            load.start()

    @pl.loop(0, nz - 1)
    def _(i):
        enter(y, target(i), x * 2 + 1)

    for j in range(1, nx):
        enter(y, z, lax.rem(x + j, nx) * 2 + 1)

    at_the_end = []

    def rows_of(h):
        return pl.ds(CUTS[h], CUTS[h + 1] - CUTS[h])

    def send_y(h, g):
        group = pl.ds(g * GROUP, GROUP)
        for j in range(1, ny):
            remote(
                acc.at[group, y_peer(j), rows_of(h)], y_buf.at[group, j - 1, rows_of(h)],
                y_send_sem, y_sem.at[h, g], y_peer(j), z, t,
            ).start()

    def accumulate(g):
        @pl.loop(g * GROUP, (g + 1) * GROUP)
        def _(i):
            for load in loads(i):
                load.wait()
            acc[i] = (g_buf[i].astype(F32) + e_buf[i].astype(F32)).astype(BF16)

    accumulate(0)

    def entered(here, count):
        @pl.when(core == here)
        def _():
            pl.semaphore_wait(barrier, count)
            pl.semaphore_signal(ready, inc=1, device_id=(dp, sibling), device_id_type=MESH)

        @pl.when(core != here)
        def _():
            pl.semaphore_wait(ready, 1)

    entered(0, 2 * (ny - 1) + 1)
    send_y(0, 0)

    @pl.loop(1, nz // GROUP)
    def _(g):
        accumulate(g)
        send_y(0, g)

    for h in range(1, PARTS):

        @pl.loop(0, nz // GROUP)
        def _(g):
            send_y(h, g)

    at_the_end.append(lambda: sent(acc.at[:, pl.ds(0, ny - 1)], y_send_sem))

    def y_total(h, i):
        total = acc[i, y, rows_of(h)].astype(F32)
        for j in range(ny - 1):
            total = total + y_buf[i, j, rows_of(h)].astype(F32)
        return total

    entered(1, 2 * (nz - 1) + 2 * (nx - 1) + 1)
    own = []
    for h in range(PARTS):

        @pl.loop(0, nz // GROUP)
        def _(g):
            got(y_buf.at[pl.ds(g * GROUP, GROUP), :, rows_of(h)], y_sem.at[h, g])

            @pl.loop(g * GROUP, lax.min((g + 1) * GROUP, nz - 1))
            def _(i):
                z_send[i, rows_of(h)] = y_total(h, i).astype(BF16)
                remote(
                    z_send.at[i, rows_of(h)], z_buf.at[i, rows_of(h)], z_send_sem, z_sem.at[h], y, target(i), t
                ).start()

        own.append(y_total(h, nz - 1))
    at_the_end.append(lambda: sent(z_send, z_send_sem))

    for h in range(PARTS):
        got(z_buf.at[:, rows_of(h)], z_sem.at[h])
        total = own[h]
        for i in range(nz - 1):
            total = total + z_buf[i, rows_of(h)].astype(F32)
        a_all[z, rows_of(h)] = total.astype(BF16)
        mine = a_all.at[z, rows_of(h)]

        @pl.loop(0, nz - 1)
        def _(i):
            remote(mine, mine, a_send_sem, a_sem, y, target(i), t).start()

    at_the_end.append(lambda: sent(a_all.at[pl.ds(0, nz - 1)], a_send_sem))

    lane16 = lax.broadcasted_iota(jnp.int32, (RANK // 2, 128), 1)
    q_rows = q_init[...].astype(BF16)
    block = a_all[z]
    p_part = lax.dot_general(
        q_rows, jnp.concatenate([block, block], axis=0), (((1,), (1,)), ((), ())), preferred_element_type=F32
    )
    t_buf[t] = jnp.where(lane16 < BLOCK, p_part[: RANK // 2], p_part[RANK // 2 :])
    for j in range(1, nt):
        remote(t_buf.at[t], t_buf.at[t], t_send_sem, t_sem, y, z, t_peer(j)).start()
    at_the_end.append(lambda: sent(t_buf.at[pl.ds(0, nt - 1)], t_send_sem))
    got(t_buf.at[pl.ds(0, nt - 1)], t_sem)
    p_packed = t_buf[0]
    for j in range(1, nt):
        p_packed = p_packed + t_buf[j]
    p1_all[z] = p_packed.astype(BF16)

    @pl.loop(0, nz - 1)
    def _(i):
        remote(p1_all.at[z], p1_all.at[z], p_send_sem, p_sem, y, target(i), t).start()

    at_the_end.append(lambda: sent(p1_all.at[pl.ds(0, nz - 1)], p_send_sem))
    got(a_all.at[pl.ds(0, nz - 1)], a_sem)
    got(p1_all.at[pl.ds(0, nz - 1)], p_sem)
    a = a_all[...].reshape(nz * BLOCK, COLS)
    columns = []
    for m in range(nz // 2):
        first, second = p1_all[2 * m].astype(F32), p1_all[2 * m + 1].astype(F32)
        top = jnp.where(lane16 < BLOCK, first, pltpu.roll(second, BLOCK, 1))
        bottom = jnp.where(lane16 < BLOCK, pltpu.roll(first, BLOCK, 1), second)
        columns.append(jnp.concatenate([top, bottom], axis=0))
    p1 = jnp.concatenate(columns, axis=1).astype(BF16)

    def sum_over_y(it, q_part, gram_part):
        s_buf[it, y, :RANK] = q_part
        s_buf[it, y, RANK:] = jnp.concatenate([gram_part[8 * k : 8 * (k + 1)] for k in range(RANK // 8)], axis=1)
        for j in range(1, ny):
            remote(s_buf.at[it, y], s_buf.at[it, y], s_send_sem.at[it], s_sem.at[it], y_peer(j), z, t).start()
        at_the_end.append(lambda: sent(s_buf.at[it, pl.ds(0, ny - 1)], s_send_sem.at[it]))

    def summed_over_y(it):
        got(s_buf.at[it, pl.ds(0, ny - 1)], s_sem.at[it])
        total = s_buf[it, 0]
        for j in range(1, ny):
            total = total + s_buf[it, j]
        return total[:RANK], total[RANK:]

    sum_over_y(
        0,
        jnp.dot(p1, a, preferred_element_type=F32),
        lax.dot_general(p1, p1, (((1,), (1,)), ((), ())), preferred_element_type=F32),
    )
    right, gram = summed_over_y(0)
    diagonal, lower, _ = eliminate(gram, right, False)
    q_rows = (lower / (jnp.sqrt(diagonal) * (ny * nz))).astype(BF16)

    p_part = lax.dot_general(q_rows, a, (((1,), (1,)), ((), ())), preferred_element_type=F32)
    part_buf[0] = p_part[:, :half]
    part_buf[1] = p_part[:, half:]
    remote(part_buf.at[other], c_buf, c_send_sem.at[0], c_sem.at[0], y, z, sibling).start()
    at_the_end.append(lambda: sent(c_buf, c_send_sem.at[0]))
    got(c_buf, c_sem.at[0])
    x_buf[x] = part_buf[core] + c_buf[...]
    for j in range(1, nx):
        remote(x_buf.at[x], x_buf.at[x], x_send_sem, x_sem, y, z, lax.rem(x + j, nx) * 2 + core).start()
    at_the_end.append(lambda: sent(x_buf.at[pl.ds(0, nx - 1)], x_send_sem))
    got(x_buf.at[pl.ds(0, nx - 1)], x_sem)
    p_half = x_buf[0]
    for j in range(1, nx):
        p_half = p_half + x_buf[j]
    p2_all[y, core] = p_half
    mine = p2_all.at[y, core]
    remote(mine, mine, c_send_sem.at[1], c_sem.at[1], y, z, sibling).start()
    at_the_end.append(lambda: sent(c_buf, c_send_sem.at[1]))
    for j in range(1, ny):
        remote(mine, mine, s_send_sem.at[2], s_sem.at[2], y_peer(j), z, t).start()
    at_the_end.append(lambda: sent(p2_all.at[pl.ds(0, ny - 1), 0], s_send_sem.at[2]))
    got(p2_all.at[y, other], c_sem.at[1])
    p2 = jnp.concatenate([p2_all[y, 0], p2_all[y, 1]], axis=1)
    p2_high = p2.astype(BF16)
    p2_low = (p2 - p2_high.astype(F32)).astype(BF16)
    halves = jnp.concatenate([p2_high, p2_low], axis=0)

    def with_halves(right, contract):
        both = lax.dot_general(halves, right, (((1,), (contract,)), ((), ())), preferred_element_type=F32)
        return both[:RANK] + both[RANK:]

    sum_over_y(1, with_halves(a, 0), with_halves(p2_high, 1) + with_halves(p2_low, 1))

    def spread(yy, c):
        for b in range(half // 128):
            tile = p2_all[yy, c, :, b * 128 : (b + 1) * 128]
            high = tile.astype(BF16)
            low = (tile - high.astype(F32)).astype(BF16)
            start = yy * 2 * half + c * half + b * 128
            p_rows[pl.ds(pl.multiple_of(start, 128), 128)] = jnp.concatenate([high, low, high, low], axis=0).T

    for c in range(2):
        spread(y, c)

    got(p2_all.at[pl.ds(0, ny - 1), 0], s_sem.at[2])
    for j in range(1, ny):
        theirs = p2_all.at[y_peer(j), core]
        remote(theirs, theirs, c_send_sem.at[2], c_sem.at[2], y, z, sibling).start()
    at_the_end.append(lambda: sent(p2_all.at[pl.ds(0, ny - 1), 0], c_send_sem.at[2]))
    right, gram = summed_over_y(1)
    got(p2_all.at[pl.ds(0, ny - 1), 0], c_sem.at[2])
    for j in range(1, ny):
        for c in range(2):
            spread(y_peer(j), c)
    diagonal, lower, full = eliminate(gram, right, True)
    q_out[...] = lower / (jnp.sqrt(diagonal) * (ny * nz))
    m = full / (diagonal * (ny * nz))
    m_high = m.astype(BF16)
    m_low = (m - m_high.astype(F32)).astype(BF16)
    m_rows = jnp.concatenate([m_high, m_high, m_low, m_low], axis=0)

    @pl.loop(0, nz, unroll=4)
    def _(i):
        zt = target(i)
        left = jnp.concatenate(
            [p_rows[pl.ds(pl.multiple_of((yy * nz + zt) * BLOCK, BLOCK), BLOCK)] for yy in range(ny)], axis=0
        )
        approx = jnp.dot(left, m_rows, preferred_element_type=F32).reshape(ny, BLOCK, COLS)
        new_error[:, zt] = (acc[i].astype(F32) - approx).astype(BF16)

    for wait in at_the_end:
        wait()


def on_device(ny, nz, nt, grads, error, q_init):
    dma = pltpu.SemaphoreType.DMA
    blocks = (ny, nz, BLOCK, COLS)
    half = nz * BLOCK // 2
    new_error, q_rows = pl.pallas_call(
        functools.partial(kernel, ny, nz, nt),
        out_shape=(jax.ShapeDtypeStruct(blocks, BF16), jax.ShapeDtypeStruct((RANK, COLS), F32)),
        in_specs=[
            pl.BlockSpec(memory_space=pl.ANY),
            pl.BlockSpec(memory_space=pl.ANY),
            pl.BlockSpec(memory_space=pltpu.VMEM),
        ],
        out_specs=(pl.BlockSpec(memory_space=pltpu.VMEM), pl.BlockSpec(memory_space=pltpu.VMEM)),
        scratch_shapes=[
            pltpu.VMEM((nz, ny, BLOCK, COLS), BF16),
            pltpu.VMEM((nz, ny, BLOCK, COLS), BF16),
            pltpu.VMEM((nz, ny, BLOCK, COLS), BF16),
            pltpu.VMEM((nz, ny - 1, BLOCK, COLS), BF16),
            pltpu.VMEM((nz - 1, BLOCK, COLS), BF16),
            pltpu.VMEM((nz - 1, BLOCK, COLS), BF16),
            pltpu.VMEM((nz, BLOCK, COLS), BF16),
            pltpu.VMEM((nt, RANK // 2, 128), F32),
            pltpu.VMEM((nz, RANK // 2, 128), BF16),
            pltpu.VMEM((2, ny, SUMS, 128), F32),
            pltpu.VMEM((2, RANK, half), F32),
            pltpu.VMEM((RANK, half), F32),
            pltpu.VMEM((nt // 2, RANK, half), F32),
            pltpu.VMEM((ny, 2, RANK, half), F32),
            pltpu.VMEM((ny * nz * BLOCK, 4 * RANK), BF16),
            dma((2, nz)), dma, dma((PARTS, nz // GROUP)), dma, dma((PARTS,)), dma, dma, dma, dma, dma, dma,
            dma((3,)), dma((3,)), dma((3,)), dma((3,)), dma, dma, pltpu.SemaphoreType.REGULAR,
        ],
        compiler_params=pltpu.CompilerParams(
            collective_id=0, has_side_effects=True, vmem_limit_bytes=52 * 1024 * 1024
        ),
    )(grads.reshape(blocks), error.reshape(blocks), q_init.T)
    return new_error.reshape(1, ny * nz * BLOCK, COLS), q_rows.T


def solution(mesh, ny=4):
    nz, nt = mesh.shape["dp"] // ny, mesh.shape["tensor"]
    return jax.shard_map(
        functools.partial(on_device, ny, nz, nt),
        mesh=mesh,
        in_specs=(P("dp", None, "tensor"), P("dp", None, "tensor"), P("tensor", None)),
        out_specs=(P("dp", None, "tensor"), P("tensor", None)),
        check_vma=False,
    )
```

```python
import functools

import jax
import jax.numpy as jnp
from jax import lax
from jax.experimental import pallas as pl
from jax.experimental.pallas import tpu as pltpu
from jax.sharding import PartitionSpec as P

MESH = pl.DeviceIdType.MESH
HIGHEST = lax.Precision.HIGHEST
RANK = 32
BLOCK = 64
CUTS = (0, 32, BLOCK)
PARTS = len(CUTS) - 1
STEPS = 8
GROUP = 2
COLS = 128
SUMS = 40
F32, BF16 = jnp.float32, jnp.bfloat16


def eliminate(gram_packed, right, both_sides):
    row = lax.broadcasted_iota(jnp.int32, (8, 128), 0)
    lane = lax.broadcasted_iota(jnp.int32, (8, 128), 1)
    tiles = RANK // 8
    work = [gram_packed if r == 0 else pltpu.roll(gram_packed, 128 - RANK * r, 1) for r in range(tiles)]
    lower = [right[8 * r : 8 * (r + 1)] for r in range(tiles)]
    full = list(lower)
    diagonal = [jnp.zeros((8, 128), F32)] * tiles
    for first in range(0, RANK, STEPS):
        columns = [
            [jnp.broadcast_to(work[r][:, first + j : first + j + 1], (8, 128)) for r in range(tiles)]
            for j in range(STEPS)
        ]
        for j in range(STEPS):
            k = first + j
            own, at = k // 8, k % 8
            pivot = columns[j][own][at : at + 1]
            inverse = 1.0 / pivot
            diagonal[own] = jnp.where(row == at, pivot, diagonal[own])
            factor, below = [], []
            for r in range(tiles):
                scaled = columns[j][r] * inverse
                factor.append(jnp.where(row == at, 0.0, scaled) if r == own else scaled)
                below.append(jnp.where(row > at, scaled, 0.0) if r == own else scaled)

            def step(matrix, factors, start):
                pivot_row = matrix[own][at : at + 1]
                for r in range(start, tiles):
                    matrix[r] = matrix[r] - factors[r] * pivot_row

            both = (factor, 0) if both_sides else (below, own)
            for later in columns[j + 1 :]:
                step(later, *both)
            step(lower, below, own)
            if both_sides:
                step(full, factor, 0)
            step(work, *both)
    return tuple(jnp.concatenate(m, axis=0) for m in (diagonal, lower, full))


def kernel(
    ny, nz, nt,
    grads, error, q_init, new_error, q_out,
    g_buf, e_buf, acc, y_buf, z_send, z_buf, a_all, t_buf, p1_all, s_buf, part_buf, c_buf, x_buf, p2_all, p_rows,
    load_sem, y_send_sem, y_sem, z_send_sem, z_sem, a_send_sem, a_sem, n_send_sem, n_sem, t_send_sem, t_sem, p_send_sem, p_sem,
    s_send_sem, s_sem, c_send_sem, c_sem, x_send_sem, x_sem, ready,
):
    nx = nt // 2
    dp, t = lax.axis_index("dp"), lax.axis_index("tensor")
    y, z = lax.div(dp, nz), lax.rem(dp, nz)
    x, core = lax.div(t, 2), lax.rem(t, 2)
    other = 1 - core
    sibling = x * 2 + other
    half = nz * BLOCK // 2

    def remote(src, dst, send, recv, y_, z_, t_):
        return pltpu.make_async_remote_copy(
            src_ref=src, dst_ref=dst, send_sem=send, recv_sem=recv,
            device_id=(y_ * nz + z_, t_), device_id_type=MESH,
        )

    def got(ref, sem):
        remote(ref, ref, sem, sem, y, z, t).wait_recv()

    def sent(ref, sem):
        remote(ref, ref, sem, sem, y, z, t).wait_send()

    def y_peer(j):
        return lax.rem(y + j, ny)

    def t_peer(j):
        return lax.rem(t + j, nt)

    def target(i):
        return lax.rem(z + nz // 2 + (1 - 2 * lax.rem(i, 2)) * lax.div(i + 1, 2) + nz, nz)

    def loads(i):
        zt = target(i)
        return (
            pltpu.make_async_copy(grads.at[:, zt], g_buf.at[i], load_sem.at[0, i]),
            pltpu.make_async_copy(error.at[:, zt], e_buf.at[i], load_sem.at[1, i]),
        )

    barrier = pltpu.get_barrier_semaphore()

    def enter(y_, z_, t_):
        pl.semaphore_signal(barrier, inc=1, device_id=(y_ * nz + z_, t_), device_id_type=MESH)

    for j in range(1, ny):
        enter(y_peer(j), z, x * 2)
    enter(y, z, sibling)

    @pl.loop(0, nz)
    def _(i):
        for load in loads(i):
            load.start()

    @pl.loop(0, nz - 1)
    def _(i):
        enter(y, target(i), x * 2 + 1)

    for j in range(1, nx):
        enter(y, z, lax.rem(x + j, nx) * 2 + 1)

    at_the_end = []

    def rows_of(h):
        return pl.ds(CUTS[h], CUTS[h + 1] - CUTS[h])

    def send_y(h, g):
        group = pl.ds(g * GROUP, GROUP)
        for j in range(1, ny):
            remote(
                acc.at[group, y_peer(j), rows_of(h)], y_buf.at[group, j - 1, rows_of(h)],
                y_send_sem, y_sem.at[h, g], y_peer(j), z, t,
            ).start()

    def accumulate(g):
        @pl.loop(g * GROUP, (g + 1) * GROUP)
        def _(i):
            for load in loads(i):
                load.wait()
            acc[i] = (g_buf[i].astype(F32) + e_buf[i].astype(F32)).astype(BF16)

    accumulate(0)

    def entered(here, count):
        @pl.when(core == here)
        def _():
            pl.semaphore_wait(barrier, count)
            pl.semaphore_signal(ready, inc=1, device_id=(dp, sibling), device_id_type=MESH)

        @pl.when(core != here)
        def _():
            pl.semaphore_wait(ready, 1)

    entered(0, 2 * (ny - 1) + 1)
    send_y(0, 0)

    @pl.loop(1, nz // GROUP)
    def _(g):
        accumulate(g)
        send_y(0, g)

    for h in range(1, PARTS):

        @pl.loop(0, nz // GROUP)
        def _(g):
            send_y(h, g)

    at_the_end.append(lambda: sent(acc.at[:, pl.ds(0, ny - 1)], y_send_sem))

    def y_total(h, i):
        total = acc[i, y, rows_of(h)].astype(F32)
        for j in range(ny - 1):
            total = total + y_buf[i, j, rows_of(h)].astype(F32)
        return total

    entered(1, 2 * (nz - 1) + 2 * (nx - 1) + 1)
    own = []
    for h in range(PARTS):

        @pl.loop(0, nz // GROUP)
        def _(g):
            got(y_buf.at[pl.ds(g * GROUP, GROUP), :, rows_of(h)], y_sem.at[h, g])

            @pl.loop(g * GROUP, lax.min((g + 1) * GROUP, nz - 1))
            def _(i):
                z_send[i, rows_of(h)] = y_total(h, i).astype(BF16)
                remote(
                    z_send.at[i, rows_of(h)], z_buf.at[i, rows_of(h)], z_send_sem, z_sem.at[h], y, target(i), t
                ).start()

        own.append(y_total(h, nz - 1))
    at_the_end.append(lambda: sent(z_send, z_send_sem))

    turns = nz // 4
    turn, kind = lax.div(z, 4), lax.rem(z, 4)

    def z_near(j):
        return lax.rem(z + j + nz, nz)

    for h in range(PARTS):
        got(z_buf.at[:, rows_of(h)], z_sem.at[h])
        total = own[h]
        for i in range(nz - 1):
            total = total + z_buf[i, rows_of(h)].astype(F32)
        a_all[kind, turn, rows_of(h)] = total.astype(BF16)
        mine = a_all.at[kind, turn, rows_of(h)]
        for j in range(1, turns):
            remote(mine, mine, a_send_sem, a_sem.at[h], y, z_near(4 * j), t).start()
    at_the_end.append(lambda: sent(a_all.at[0, pl.ds(0, turns - 1)], a_send_sem))

    lane16 = lax.broadcasted_iota(jnp.int32, (RANK // 2, 128), 1)
    q_rows = q_init[...].astype(BF16)
    block = a_all[kind, turn]
    p_part = lax.dot_general(
        q_rows, jnp.concatenate([block, block], axis=0), (((1,), (1,)), ((), ())), preferred_element_type=F32
    )
    t_buf[t] = jnp.where(lane16 < BLOCK, p_part[: RANK // 2], p_part[RANK // 2 :])
    for j in range(1, nt):
        remote(t_buf.at[t], t_buf.at[t], t_send_sem, t_sem, y, z, t_peer(j)).start()
    at_the_end.append(lambda: sent(t_buf.at[pl.ds(0, nt - 1)], t_send_sem))
    got(t_buf.at[pl.ds(0, nt - 1)], t_sem)
    p_packed = t_buf[0]
    for j in range(1, nt):
        p_packed = p_packed + t_buf[j]
    p1_own = p1_all.at[kind * turns + turn]
    p1_own[...] = p_packed.astype(BF16)

    @pl.loop(0, nz - 1)
    def _(i):
        remote(p1_own, p1_own, p_send_sem, p_sem, y, target(i), t).start()

    at_the_end.append(lambda: sent(p1_all.at[pl.ds(0, nz - 1)], p_send_sem))
    for h in range(PARTS):
        got(a_all.at[0, pl.ds(0, turns - 1), rows_of(h)], a_sem.at[h])
        for near, first, count in ((2, 0, turns // 2), (-2, turns // 2, turns // 2), (1, 0, turns), (-1, 0, turns)):
            some = a_all.at[kind, pl.ds(first, count), rows_of(h)]
            remote(some, some, n_send_sem, n_sem, y, z_near(near), t).start()
    at_the_end.append(lambda: sent(a_all.at[pl.ds(0, 3)], n_send_sem))
    got(a_all.at[pl.ds(0, 3)], n_sem)
    got(p1_all.at[pl.ds(0, nz - 1)], p_sem)
    a = a_all[...].reshape(nz * BLOCK, COLS)
    columns = []
    for m in range(nz // 2):
        first, second = p1_all[2 * m].astype(F32), p1_all[2 * m + 1].astype(F32)
        top = jnp.where(lane16 < BLOCK, first, pltpu.roll(second, BLOCK, 1))
        bottom = jnp.where(lane16 < BLOCK, pltpu.roll(first, BLOCK, 1), second)
        columns.append(jnp.concatenate([top, bottom], axis=0))
    p1 = jnp.concatenate(columns, axis=1).astype(BF16)

    def sum_over_y(it, q_part, gram_part):
        s_buf[it, y, :RANK] = q_part
        s_buf[it, y, RANK:] = jnp.concatenate([gram_part[8 * k : 8 * (k + 1)] for k in range(RANK // 8)], axis=1)
        for j in range(1, ny):
            remote(s_buf.at[it, y], s_buf.at[it, y], s_send_sem.at[it], s_sem.at[it], y_peer(j), z, t).start()
        at_the_end.append(lambda: sent(s_buf.at[it, pl.ds(0, ny - 1)], s_send_sem.at[it]))

    def summed_over_y(it):
        got(s_buf.at[it, pl.ds(0, ny - 1)], s_sem.at[it])
        total = s_buf[it, 0]
        for j in range(1, ny):
            total = total + s_buf[it, j]
        return total[:RANK], total[RANK:]

    sum_over_y(
        0,
        jnp.dot(p1, a, preferred_element_type=F32),
        lax.dot_general(p1, p1, (((1,), (1,)), ((), ())), preferred_element_type=F32),
    )
    right, gram = summed_over_y(0)
    diagonal, lower, _ = eliminate(gram, right, False)
    q_rows = (lower / (jnp.sqrt(diagonal) * (ny * nz))).astype(BF16)

    p_part = lax.dot_general(q_rows, a, (((1,), (1,)), ((), ())), preferred_element_type=F32)
    part_buf[0] = p_part[:, :half]
    part_buf[1] = p_part[:, half:]
    remote(part_buf.at[other], c_buf, c_send_sem.at[0], c_sem.at[0], y, z, sibling).start()
    at_the_end.append(lambda: sent(c_buf, c_send_sem.at[0]))
    got(c_buf, c_sem.at[0])
    x_buf[x] = part_buf[core] + c_buf[...]
    for j in range(1, nx):
        remote(x_buf.at[x], x_buf.at[x], x_send_sem, x_sem, y, z, lax.rem(x + j, nx) * 2 + core).start()
    at_the_end.append(lambda: sent(x_buf.at[pl.ds(0, nx - 1)], x_send_sem))
    got(x_buf.at[pl.ds(0, nx - 1)], x_sem)
    p_half = x_buf[0]
    for j in range(1, nx):
        p_half = p_half + x_buf[j]
    p2_all[y, core] = p_half
    mine = p2_all.at[y, core]
    remote(mine, mine, c_send_sem.at[1], c_sem.at[1], y, z, sibling).start()
    at_the_end.append(lambda: sent(c_buf, c_send_sem.at[1]))
    for j in range(1, ny):
        remote(mine, mine, s_send_sem.at[2], s_sem.at[2], y_peer(j), z, t).start()
    at_the_end.append(lambda: sent(p2_all.at[pl.ds(0, ny - 1), 0], s_send_sem.at[2]))
    got(p2_all.at[y, other], c_sem.at[1])
    p2 = jnp.concatenate([p2_all[y, 0], p2_all[y, 1]], axis=1)
    p2_high = p2.astype(BF16)
    p2_low = (p2 - p2_high.astype(F32)).astype(BF16)
    halves = jnp.concatenate([p2_high, p2_low], axis=0)

    def with_halves(right, contract):
        both = lax.dot_general(halves, right, (((1,), (contract,)), ((), ())), preferred_element_type=F32)
        return both[:RANK] + both[RANK:]

    sum_over_y(1, with_halves(a, 0), with_halves(p2_high, 1) + with_halves(p2_low, 1))

    def spread(yy, c):
        for b in range(half // 128):
            tile = p2_all[yy, c, :, b * 128 : (b + 1) * 128]
            high = tile.astype(BF16)
            low = (tile - high.astype(F32)).astype(BF16)
            start = yy * 2 * half + c * half + b * 128
            p_rows[pl.ds(pl.multiple_of(start, 128), 128)] = jnp.concatenate([high, low, high, low], axis=0).T

    for c in range(2):
        spread(y, c)

    got(p2_all.at[pl.ds(0, ny - 1), 0], s_sem.at[2])
    for j in range(1, ny):
        theirs = p2_all.at[y_peer(j), core]
        remote(theirs, theirs, c_send_sem.at[2], c_sem.at[2], y, z, sibling).start()
    at_the_end.append(lambda: sent(p2_all.at[pl.ds(0, ny - 1), 0], c_send_sem.at[2]))
    right, gram = summed_over_y(1)
    got(p2_all.at[pl.ds(0, ny - 1), 0], c_sem.at[2])
    for j in range(1, ny):
        for c in range(2):
            spread(y_peer(j), c)
    diagonal, lower, full = eliminate(gram, right, True)
    q_out[...] = lower / (jnp.sqrt(diagonal) * (ny * nz))
    m = full / (diagonal * (ny * nz))
    m_high = m.astype(BF16)
    m_low = (m - m_high.astype(F32)).astype(BF16)
    m_rows = jnp.concatenate([m_high, m_high, m_low, m_low], axis=0)

    @pl.loop(0, nz, unroll=4)
    def _(i):
        zt = target(i)
        place = lax.rem(zt, 4) * (nz // 4) + lax.div(zt, 4)
        left = jnp.concatenate(
            [p_rows[pl.ds(pl.multiple_of((yy * nz + place) * BLOCK, BLOCK), BLOCK)] for yy in range(ny)], axis=0
        )
        approx = jnp.dot(left, m_rows, preferred_element_type=F32).reshape(ny, BLOCK, COLS)
        new_error[:, zt] = (acc[i].astype(F32) - approx).astype(BF16)

    for wait in at_the_end:
        wait()


def on_device(ny, nz, nt, grads, error, q_init):
    dma = pltpu.SemaphoreType.DMA
    blocks = (ny, nz, BLOCK, COLS)
    half = nz * BLOCK // 2
    new_error, q_rows = pl.pallas_call(
        functools.partial(kernel, ny, nz, nt),
        out_shape=(jax.ShapeDtypeStruct(blocks, BF16), jax.ShapeDtypeStruct((RANK, COLS), F32)),
        in_specs=[
            pl.BlockSpec(memory_space=pl.ANY),
            pl.BlockSpec(memory_space=pl.ANY),
            pl.BlockSpec(memory_space=pltpu.VMEM),
        ],
        out_specs=(pl.BlockSpec(memory_space=pltpu.VMEM), pl.BlockSpec(memory_space=pltpu.VMEM)),
        scratch_shapes=[
            pltpu.VMEM((nz, ny, BLOCK, COLS), BF16),
            pltpu.VMEM((nz, ny, BLOCK, COLS), BF16),
            pltpu.VMEM((nz, ny, BLOCK, COLS), BF16),
            pltpu.VMEM((nz, ny - 1, BLOCK, COLS), BF16),
            pltpu.VMEM((nz - 1, BLOCK, COLS), BF16),
            pltpu.VMEM((nz - 1, BLOCK, COLS), BF16),
            pltpu.VMEM((4, nz // 4, BLOCK, COLS), BF16),
            pltpu.VMEM((nt, RANK // 2, 128), F32),
            pltpu.VMEM((nz, RANK // 2, 128), BF16),
            pltpu.VMEM((2, ny, SUMS, 128), F32),
            pltpu.VMEM((2, RANK, half), F32),
            pltpu.VMEM((RANK, half), F32),
            pltpu.VMEM((nt // 2, RANK, half), F32),
            pltpu.VMEM((ny, 2, RANK, half), F32),
            pltpu.VMEM((ny * nz * BLOCK, 4 * RANK), BF16),
            dma((2, nz)), dma, dma((PARTS, nz // GROUP)), dma, dma((PARTS,)), dma, dma((PARTS,)), dma, dma, dma, dma, dma, dma,
            dma((3,)), dma((3,)), dma((3,)), dma((3,)), dma, dma, pltpu.SemaphoreType.REGULAR,
        ],
        compiler_params=pltpu.CompilerParams(
            collective_id=0, has_side_effects=True, vmem_limit_bytes=52 * 1024 * 1024
        ),
    )(grads.reshape(blocks), error.reshape(blocks), q_init.T)
    return new_error.reshape(1, ny * nz * BLOCK, COLS), q_rows.T


def solution(mesh, ny=4):
    nz, nt = mesh.shape["dp"] // ny, mesh.shape["tensor"]
    return jax.shard_map(
        functools.partial(on_device, ny, nz, nt),
        mesh=mesh,
        in_specs=(P("dp", None, "tensor"), P("dp", None, "tensor"), P("tensor", None)),
        out_specs=(P("dp", None, "tensor"), P("tensor", None)),
        check_vma=False,
    )
```

```python
import functools

import jax
import jax.numpy as jnp
from jax import lax
from jax.experimental import pallas as pl
from jax.experimental.pallas import tpu as pltpu
from jax.sharding import PartitionSpec as P

MESH = pl.DeviceIdType.MESH
HIGHEST = lax.Precision.HIGHEST
RANK = 32
BLOCK = 64
CUTS = (0, 32, BLOCK)
PARTS = len(CUTS) - 1
STEPS = 8
GROUP = 2
COLS = 128
SUMS = 40
F32, BF16 = jnp.float32, jnp.bfloat16


def eliminate(gram_packed, right, both_sides):
    row = lax.broadcasted_iota(jnp.int32, (8, 128), 0)
    lane = lax.broadcasted_iota(jnp.int32, (8, 128), 1)
    tiles = RANK // 8
    work = [gram_packed if r == 0 else pltpu.roll(gram_packed, 128 - RANK * r, 1) for r in range(tiles)]
    lower = [right[8 * r : 8 * (r + 1)] for r in range(tiles)]
    full = list(lower)
    diagonal = [jnp.zeros((8, 128), F32)] * tiles
    for first in range(0, RANK, STEPS):
        columns = [
            [jnp.broadcast_to(work[r][:, first + j : first + j + 1], (8, 128)) for r in range(tiles)]
            for j in range(STEPS)
        ]
        for j in range(STEPS):
            k = first + j
            own, at = k // 8, k % 8
            pivot = columns[j][own][at : at + 1]
            inverse = 1.0 / pivot
            diagonal[own] = jnp.where(row == at, pivot, diagonal[own])
            factor, below = [], []
            for r in range(tiles):
                scaled = columns[j][r] * inverse
                factor.append(jnp.where(row == at, 0.0, scaled) if r == own else scaled)
                below.append(jnp.where(row > at, scaled, 0.0) if r == own else scaled)

            def step(matrix, factors, start):
                pivot_row = matrix[own][at : at + 1]
                for r in range(start, tiles):
                    matrix[r] = matrix[r] - factors[r] * pivot_row

            both = (factor, 0) if both_sides else (below, own)
            for later in columns[j + 1 :]:
                step(later, *both)
            step(lower, below, own)
            if both_sides:
                step(full, factor, 0)
            step(work, *both)
    return tuple(jnp.concatenate(m, axis=0) for m in (diagonal, lower, full))


def kernel(
    ny, nz, nt,
    grads, error, q_init, new_error, q_out,
    g_buf, e_buf, acc, y_buf, z_send, z_buf, a_all, t_buf, p1_all, s_buf, part_buf, c_buf, x_buf, p2_all, p_rows,
    load_sem, y_send_sem, y_sem, z_send_sem, z_sem, a_send_sem, a_sem, n_send_sem, n_sem, t_send_sem, t_sem, p_send_sem, p_sem,
    s_send_sem, s_sem, c_send_sem, c_sem, x_send_sem, x_sem, ready,
):
    nx = nt // 2
    dp, t = lax.axis_index("dp"), lax.axis_index("tensor")
    y, z = lax.div(dp, nz), lax.rem(dp, nz)
    x, core = lax.div(t, 2), lax.rem(t, 2)
    other = 1 - core
    sibling = x * 2 + other
    half = nz * BLOCK // 2

    def remote(src, dst, send, recv, y_, z_, t_):
        return pltpu.make_async_remote_copy(
            src_ref=src, dst_ref=dst, send_sem=send, recv_sem=recv,
            device_id=(y_ * nz + z_, t_), device_id_type=MESH,
        )

    def got(ref, sem):
        remote(ref, ref, sem, sem, y, z, t).wait_recv()

    def sent(ref, sem):
        remote(ref, ref, sem, sem, y, z, t).wait_send()

    def y_peer(j):
        return lax.rem(y + j, ny)

    def t_peer(j):
        return lax.rem(t + j, nt)

    def target(i):
        return lax.rem(z + nz // 2 + (1 - 2 * lax.rem(i, 2)) * lax.div(i + 1, 2) + nz, nz)

    def loads(i):
        zt = target(i)
        return (
            pltpu.make_async_copy(grads.at[:, zt], g_buf.at[i], load_sem.at[0, i]),
            pltpu.make_async_copy(error.at[:, zt], e_buf.at[i], load_sem.at[1, i]),
        )

    barrier = pltpu.get_barrier_semaphore()

    def enter(y_, z_, t_):
        pl.semaphore_signal(barrier, inc=1, device_id=(y_ * nz + z_, t_), device_id_type=MESH)

    for j in range(1, ny):
        enter(y_peer(j), z, x * 2)
    enter(y, z, sibling)

    @pl.loop(0, nz)
    def _(i):
        for load in loads(i):
            load.start()

    @pl.loop(0, nz - 1)
    def _(i):
        enter(y, target(i), x * 2 + 1)

    for j in range(1, nx):
        enter(y, z, lax.rem(x + j, nx) * 2 + 1)

    at_the_end = []

    def all_sent():
        while at_the_end:
            at_the_end.pop(0)()

    def rows_of(h):
        return pl.ds(CUTS[h], CUTS[h + 1] - CUTS[h])

    def send_y(h, g):
        group = pl.ds(g * GROUP, GROUP)
        for j in range(1, ny):
            remote(
                acc.at[group, y_peer(j), rows_of(h)], y_buf.at[group, j - 1, rows_of(h)],
                y_send_sem, y_sem.at[h, g], y_peer(j), z, t,
            ).start()

    def accumulate(g):
        @pl.loop(g * GROUP, (g + 1) * GROUP)
        def _(i):
            for load in loads(i):
                load.wait()
            acc[i] = (g_buf[i].astype(F32) + e_buf[i].astype(F32)).astype(BF16)

    accumulate(0)

    def entered(here, count):
        @pl.when(core == here)
        def _():
            pl.semaphore_wait(barrier, count)
            pl.semaphore_signal(ready, inc=1, device_id=(dp, sibling), device_id_type=MESH)

        @pl.when(core != here)
        def _():
            pl.semaphore_wait(ready, 1)

    entered(0, 2 * (ny - 1) + 1)
    send_y(0, 0)

    @pl.loop(1, nz // GROUP)
    def _(g):
        accumulate(g)
        send_y(0, g)

    for h in range(1, PARTS):

        @pl.loop(0, nz // GROUP)
        def _(g):
            send_y(h, g)

    at_the_end.append(lambda: sent(acc.at[:, pl.ds(0, ny - 1)], y_send_sem))

    def y_total(h, i):
        total = acc[i, y, rows_of(h)].astype(F32)
        for j in range(ny - 1):
            total = total + y_buf[i, j, rows_of(h)].astype(F32)
        return total

    entered(1, 2 * (nz - 1) + 2 * (nx - 1) + 1)
    own = []
    for h in range(PARTS):

        @pl.loop(0, nz // GROUP)
        def _(g):
            got(y_buf.at[pl.ds(g * GROUP, GROUP), :, rows_of(h)], y_sem.at[h, g])

            @pl.loop(g * GROUP, lax.min((g + 1) * GROUP, nz - 1))
            def _(i):
                z_send[i, rows_of(h)] = y_total(h, i).astype(BF16)
                remote(
                    z_send.at[i, rows_of(h)], z_buf.at[i, rows_of(h)], z_send_sem, z_sem.at[h], y, target(i), t
                ).start()

        own.append(y_total(h, nz - 1))
    at_the_end.append(lambda: sent(z_send, z_send_sem))

    turns = nz // 4
    turn, kind = lax.div(z, 4), lax.rem(z, 4)

    def z_near(j):
        return lax.rem(z + j + nz, nz)

    for h in range(PARTS):
        got(z_buf.at[:, rows_of(h)], z_sem.at[h])
        total = own[h]
        for i in range(nz - 1):
            total = total + z_buf[i, rows_of(h)].astype(F32)
        a_all[kind, turn, rows_of(h)] = total.astype(BF16)
        mine = a_all.at[kind, turn, rows_of(h)]
        for j in range(1, turns):
            remote(mine, mine, a_send_sem, a_sem.at[h], y, z_near(4 * j), t).start()
    at_the_end.append(lambda: sent(a_all.at[0, pl.ds(0, turns - 1)], a_send_sem))

    lane16 = lax.broadcasted_iota(jnp.int32, (RANK // 2, 128), 1)
    q_rows = q_init[...].astype(BF16)
    block = a_all[kind, turn]
    p_part = lax.dot_general(
        q_rows, jnp.concatenate([block, block], axis=0), (((1,), (1,)), ((), ())), preferred_element_type=F32
    )
    t_buf[t] = jnp.where(lane16 < BLOCK, p_part[: RANK // 2], p_part[RANK // 2 :])
    for j in range(1, nt):
        remote(t_buf.at[t], t_buf.at[t], t_send_sem, t_sem, y, z, t_peer(j)).start()
    at_the_end.append(lambda: sent(t_buf.at[pl.ds(0, nt - 1)], t_send_sem))
    got(t_buf.at[pl.ds(0, nt - 1)], t_sem)
    p_packed = t_buf[0]
    for j in range(1, nt):
        p_packed = p_packed + t_buf[j]
    p1_own = p1_all.at[kind * turns + turn]
    p1_own[...] = p_packed.astype(BF16)

    @pl.loop(0, nz - 1)
    def _(i):
        remote(p1_own, p1_own, p_send_sem, p_sem, y, target(i), t).start()

    at_the_end.append(lambda: sent(p1_all.at[pl.ds(0, nz - 1)], p_send_sem))
    for h in range(PARTS):
        got(a_all.at[0, pl.ds(0, turns - 1), rows_of(h)], a_sem.at[h])
        for near, first, count in ((2, 0, turns // 2), (-2, turns // 2, turns // 2), (1, 0, turns), (-1, 0, turns)):
            some = a_all.at[kind, pl.ds(first, count), rows_of(h)]
            remote(some, some, n_send_sem, n_sem, y, z_near(near), t).start()
    at_the_end.append(lambda: sent(a_all.at[pl.ds(0, 3)], n_send_sem))
    got(a_all.at[pl.ds(0, 3)], n_sem)
    got(p1_all.at[pl.ds(0, nz - 1)], p_sem)
    a = a_all[...].reshape(nz * BLOCK, COLS)
    columns = []
    for m in range(nz // 2):
        first, second = p1_all[2 * m].astype(F32), p1_all[2 * m + 1].astype(F32)
        top = jnp.where(lane16 < BLOCK, first, pltpu.roll(second, BLOCK, 1))
        bottom = jnp.where(lane16 < BLOCK, pltpu.roll(first, BLOCK, 1), second)
        columns.append(jnp.concatenate([top, bottom], axis=0))
    p1 = jnp.concatenate(columns, axis=1).astype(BF16)

    def sum_over_y(it, q_part, gram_part):
        s_buf[it, y, :RANK] = q_part
        s_buf[it, y, RANK:] = jnp.concatenate([gram_part[8 * k : 8 * (k + 1)] for k in range(RANK // 8)], axis=1)
        for j in range(1, ny):
            remote(s_buf.at[it, y], s_buf.at[it, y], s_send_sem.at[it], s_sem.at[it], y_peer(j), z, t).start()
        at_the_end.append(lambda: sent(s_buf.at[it, pl.ds(0, ny - 1)], s_send_sem.at[it]))

    def summed_over_y(it):
        got(s_buf.at[it, pl.ds(0, ny - 1)], s_sem.at[it])
        total = s_buf[it, 0]
        for j in range(1, ny):
            total = total + s_buf[it, j]
        return total[:RANK], total[RANK:]

    before = list(at_the_end)
    at_the_end.clear()
    sum_over_y(
        0,
        jnp.dot(p1, a, preferred_element_type=F32),
        lax.dot_general(p1, p1, (((1,), (1,)), ((), ())), preferred_element_type=F32),
    )
    for wait in before:
        wait()
    right, gram = summed_over_y(0)
    diagonal, lower, _ = eliminate(gram, right, False)
    q_rows = (lower / (jnp.sqrt(diagonal) * (ny * nz))).astype(BF16)

    p_part = lax.dot_general(q_rows, a, (((1,), (1,)), ((), ())), preferred_element_type=F32)
    part_buf[0] = p_part[:, :half]
    part_buf[1] = p_part[:, half:]
    remote(part_buf.at[other], c_buf, c_send_sem.at[0], c_sem.at[0], y, z, sibling).start()
    at_the_end.append(lambda: sent(c_buf, c_send_sem.at[0]))
    got(c_buf, c_sem.at[0])
    x_buf[x] = (part_buf[core] + c_buf[...]).astype(BF16)
    for j in range(1, nx):
        remote(x_buf.at[x], x_buf.at[x], x_send_sem, x_sem, y, z, lax.rem(x + j, nx) * 2 + core).start()
    all_sent()
    at_the_end.append(lambda: sent(x_buf.at[pl.ds(0, nx - 1)], x_send_sem))
    got(x_buf.at[pl.ds(0, nx - 1)], x_sem)
    before = list(at_the_end)
    at_the_end.clear()
    p_half = x_buf[0].astype(F32)
    for j in range(1, nx):
        p_half = p_half + x_buf[j].astype(F32)
    p2_all[y, core] = p_half.astype(BF16)
    mine = p2_all.at[y, core]
    remote(mine, mine, c_send_sem.at[1], c_sem.at[1], y, z, sibling).start()
    at_the_end.append(lambda: sent(mine, c_send_sem.at[1]))
    for j in range(1, ny):
        remote(mine, mine, s_send_sem.at[2], s_sem.at[2], y_peer(j), z, t).start()
    at_the_end.append(lambda: sent(p2_all.at[pl.ds(0, ny - 1), 0], s_send_sem.at[2]))
    got(p2_all.at[y, other], c_sem.at[1])
    p2 = jnp.concatenate([p2_all[y, 0], p2_all[y, 1]], axis=1)
    sum_over_y(
        1,
        jnp.dot(p2, a, preferred_element_type=F32),
        lax.dot_general(p2, p2, (((1,), (1,)), ((), ())), preferred_element_type=F32),
    )

    def spread(yy, c):
        for b in range(half // 128):
            tile = p2_all[yy, c, :, b * 128 : (b + 1) * 128]
            start = yy * 2 * half + c * half + b * 128
            p_rows[pl.ds(pl.multiple_of(start, 128), 128)] = jnp.concatenate([tile] * 4, axis=0).T

    for c in range(2):
        spread(y, c)
    for wait in before:
        wait()

    got(p2_all.at[pl.ds(0, ny - 1), 0], s_sem.at[2])
    for j in range(1, ny):
        theirs = p2_all.at[y_peer(j), core]
        remote(theirs, theirs, c_send_sem.at[2], c_sem.at[2], y, z, sibling).start()
    at_the_end.append(lambda: sent(p2_all.at[pl.ds(0, ny - 1), 0], c_send_sem.at[2]))
    right, gram = summed_over_y(1)
    got(p2_all.at[pl.ds(0, ny - 1), 0], c_sem.at[2])
    for j in range(1, ny):
        for c in range(2):
            spread(y_peer(j), c)
    diagonal, lower, full = eliminate(gram, right, True)
    q_out[...] = lower / (jnp.sqrt(diagonal) * (ny * nz))
    m = full / (diagonal * (ny * nz))
    m_high = m.astype(BF16)
    m_low = (m - m_high.astype(F32)).astype(BF16)
    m_rows = jnp.concatenate([m_high, m_low, jnp.zeros_like(m_high), jnp.zeros_like(m_high)], axis=0)

    @pl.loop(0, nz, unroll=4)
    def _(i):
        zt = target(i)
        place = lax.rem(zt, 4) * (nz // 4) + lax.div(zt, 4)
        left = jnp.concatenate(
            [p_rows[pl.ds(pl.multiple_of((yy * nz + place) * BLOCK, BLOCK), BLOCK)] for yy in range(ny)], axis=0
        )
        approx = jnp.dot(left, m_rows, preferred_element_type=F32).reshape(ny, BLOCK, COLS)
        new_error[:, zt] = (acc[i].astype(F32) - approx).astype(BF16)

    all_sent()


def on_device(ny, nz, nt, grads, error, q_init):
    dma = pltpu.SemaphoreType.DMA
    blocks = (ny, nz, BLOCK, COLS)
    half = nz * BLOCK // 2
    new_error, q_rows = pl.pallas_call(
        functools.partial(kernel, ny, nz, nt),
        out_shape=(jax.ShapeDtypeStruct(blocks, BF16), jax.ShapeDtypeStruct((RANK, COLS), F32)),
        in_specs=[
            pl.BlockSpec(memory_space=pl.ANY),
            pl.BlockSpec(memory_space=pl.ANY),
            pl.BlockSpec(memory_space=pltpu.VMEM),
        ],
        out_specs=(pl.BlockSpec(memory_space=pltpu.VMEM), pl.BlockSpec(memory_space=pltpu.VMEM)),
        scratch_shapes=[
            pltpu.VMEM((nz, ny, BLOCK, COLS), BF16),
            pltpu.VMEM((nz, ny, BLOCK, COLS), BF16),
            pltpu.VMEM((nz, ny, BLOCK, COLS), BF16),
            pltpu.VMEM((nz, ny - 1, BLOCK, COLS), BF16),
            pltpu.VMEM((nz - 1, BLOCK, COLS), BF16),
            pltpu.VMEM((nz - 1, BLOCK, COLS), BF16),
            pltpu.VMEM((4, nz // 4, BLOCK, COLS), BF16),
            pltpu.VMEM((nt, RANK // 2, 128), F32),
            pltpu.VMEM((nz, RANK // 2, 128), BF16),
            pltpu.VMEM((2, ny, SUMS, 128), F32),
            pltpu.VMEM((2, RANK, half), F32),
            pltpu.VMEM((RANK, half), F32),
            pltpu.VMEM((nt // 2, RANK, half), BF16),
            pltpu.VMEM((ny, 2, RANK, half), BF16),
            pltpu.VMEM((ny * nz * BLOCK, 4 * RANK), BF16),
            dma((2, nz)), dma, dma((PARTS, nz // GROUP)), dma, dma((PARTS,)), dma, dma((PARTS,)), dma, dma, dma, dma, dma, dma,
            dma((3,)), dma((3,)), dma((3,)), dma((3,)), dma, dma, pltpu.SemaphoreType.REGULAR,
        ],
        compiler_params=pltpu.CompilerParams(
            collective_id=0, has_side_effects=True, vmem_limit_bytes=52 * 1024 * 1024
        ),
    )(grads.reshape(blocks), error.reshape(blocks), q_init.T)
    return new_error.reshape(1, ny * nz * BLOCK, COLS), q_rows.T


def solution(mesh, ny=4):
    nz, nt = mesh.shape["dp"] // ny, mesh.shape["tensor"]
    return jax.shard_map(
        functools.partial(on_device, ny, nz, nt),
        mesh=mesh,
        in_specs=(P("dp", None, "tensor"), P("dp", None, "tensor"), P("tensor", None)),
        out_specs=(P("dp", None, "tensor"), P("tensor", None)),
        check_vma=False,
    )
```
